512 devices in a mesh: pp: 8 (over z), sp: 64 (over y, x, core).
Axes of the slice: x: 4, y: 8, z: 8, core: 2. Of those that a mesh axis runs over, the one named last changes fastest.
Arguments:
- queries: bfloat16 [8, 8192, 4096], P('pp', 'sp'), may hold values from -8 to 8
- keys: bfloat16 [8, 8192, 512], P('pp', 'sp'), may hold values from -8 to 8
- values: bfloat16 [8, 8192, 512], P('pp', 'sp'), may hold values from -6 to 6
- doc_ids: int32 [8, 8192], P('pp', 'sp'), may hold values from 0 to 7, never falling along the last dimension, each value on 1 to 2048 neighbouring positions
Outputs:
- handed: bfloat16 [8, 8192, 4096], P('pp', 'sp')
The draws below stay inside these ranges and needn't reach their ends.
Inputs may be any that keep to these rules, and one draw needn't show every extreme that they name: `doc_ids`: ids never fall along a micro-batch, each document has 1 to 2048 tokens, and one has exactly 2048.
All inputs are finite; a program needn't handle non-finite values.
Results may differ from the reference program's by a relative error of at most 0.008.
Values may be sent and summed in bfloat16 or wider, within the bound.
No kernel may reach another device: no remote copies, remote signals or barrier semaphores. Data moves between devices by JAX's collectives and lax.ppermute only.
A program may use at most 64 MiB of HBM per device.

```python
import math
import jax
import jax.numpy as jnp
import numpy as np
from jax import lax

HQ = 32
HK = 4
HEAD = 128
MOST_DOC = 2048
TOKENS = 8192
DOCS = 8
N_PP = 8


def draw_queries(key, part):
    key = jax.random.fold_in(key, 11)
    base = jax.random.normal(key, (N_PP, TOKENS, HQ * HEAD), jnp.float32)
    return jnp.clip(base, -8.0, 8.0).astype(jnp.bfloat16)


def draw_keys(key, part):
    key = jax.random.fold_in(key, 23)
    base = jax.random.normal(key, (N_PP, TOKENS, HK * HEAD), jnp.float32)
    return jnp.clip(base, -8.0, 8.0).astype(jnp.bfloat16)


def levels(stream_key, dims, cuts, low, high):
    level, own = 1.0, jax.random.fold_in(stream_key, 6)
    for dim, blocks in cuts:
        steps = jnp.exp(jax.random.uniform(jax.random.fold_in(own, dim), (blocks,), jnp.float32, low / len(cuts), high / len(cuts)))
        level = level * jnp.repeat(steps, dims[dim] // blocks).reshape([-1 if axis == dim else 1 for axis in range(len(dims))])
    return level


def profile(amount, total, most, lean):
    loads = [(1 << 20) // math.isqrt(grade ** lean) + 1 for grade in range(2, amount + 1)]
    surplus, holding = total - most - (amount - 1), [1] * (amount - 1)
    while surplus > 0:
        free = [i for i in range(amount - 1) if holding[i] < most]
        whole, budget = sum([loads[i] for i in free]), surplus
        for i in free:
            more = min(most - holding[i], max(1, budget * loads[i] // whole), surplus)
            holding[i] = holding[i] + more
            surplus = surplus - more
    return np.array([most] + holding)


def uneven_parts(own_key, number_of, total, limit, skew):
    if number_of == 2:
        one = jax.random.randint(own_key, (), max(1, total - limit), min(limit, total - 1) + 1)
        return jnp.stack([one, total - one])
    lengths = jnp.asarray(profile(number_of, total, limit, skew), jnp.int32)
    twos = (number_of - 1) // 2
    donor, sink = lengths[1:1 + 2 * twos:2], lengths[2:2 + 2 * twos:2]
    slack = jnp.minimum(donor - 1, limit - sink)
    passed = jax.random.randint(jax.random.fold_in(own_key, 1), (twos,), 0, 1 << 20) % (slack + 1)
    lengths = lengths.at[1:1 + 2 * twos:2].set(donor - passed).at[2:2 + 2 * twos:2].set(sink + passed)
    return lengths[jax.random.permutation(jax.random.fold_in(own_key, 2), number_of)]


def scatter_about(rng, shape, scale, bound, pieces=(), kind=jnp.bfloat16):
    drawn = jax.random.normal(rng, shape, jnp.float32) * scale
    if len(pieces) > 0:
        drawn = levels(rng, shape, pieces, -0.22, 0.18) * drawn
    return jnp.clip(drawn, min=-bound, max=bound).astype(kind)


def setup_inputs(seed: int = 0) -> dict:
    key_of = jax.random.split(jax.random.key(seed), 5)
    queries = draw_queries(jax.random.fold_in(key_of[4], 71), 0)
    keys = draw_keys(jax.random.fold_in(key_of[4], 71), 0)
    values = scatter_about(key_of[2], (N_PP, TOKENS, HK * HEAD), 1.0, 6.0, ((0, 8), (1, 64)))
    doc_ids = jax.vmap(lambda own: jnp.searchsorted(jnp.cumsum(uneven_parts(own, DOCS, TOKENS, MOST_DOC, 2)), jnp.arange(TOKENS), side="right"))(jax.random.split(key_of[3], N_PP)).reshape((N_PP, TOKENS)).astype(jnp.int32)
    return dict(queries=queries, keys=keys, values=values, doc_ids=doc_ids)


def attend_batch(args):
    queries, keys, values, doc_ids = args
    block_rows = min(512, TOKENS)
    group = HQ // HK
    scale = 1.0 / (HEAD ** 0.5)
    key_pad = jnp.concatenate([jnp.zeros((MOST_DOC, HK * HEAD), keys.dtype), keys], axis=0)
    val_pad = jnp.concatenate([jnp.zeros((MOST_DOC, HK * HEAD), values.dtype), values], axis=0)
    ids_pad = jnp.concatenate([jnp.full((MOST_DOC,), -1, jnp.int32), doc_ids.astype(jnp.int32)], axis=0)

    def one_block(number):
        start = (number * block_rows).astype(jnp.int32)
        width = block_rows + MOST_DOC
        qblock = lax.dynamic_slice_in_dim(queries, start, block_rows, 0)
        qblock = qblock.reshape(block_rows, HK, group, HEAD).astype(jnp.float32)
        kblock = lax.dynamic_slice_in_dim(key_pad, start, width, 0).reshape(width, HK, HEAD).astype(jnp.float32)
        vblock = lax.dynamic_slice_in_dim(val_pad, start, width, 0).reshape(width, HK, HEAD).astype(jnp.float32)
        qids = lax.dynamic_slice_in_dim(doc_ids.astype(jnp.int32), start, block_rows, 0)
        kids = lax.dynamic_slice_in_dim(ids_pad, start, width, 0)
        qpos = start + jnp.arange(block_rows, dtype=jnp.int32)
        kpos = start - MOST_DOC + jnp.arange(width, dtype=jnp.int32)
        allowed = (qids[:, None] == kids[None, :]) & (kpos[None, :] <= qpos[:, None])
        scores = jnp.einsum('tkgd,skd->kgts', qblock, kblock) * scale
        masked = jnp.where(allowed, scores, -jnp.inf)
        top = jnp.max(masked, axis=-1, keepdims=True)
        weight = jnp.where(allowed, jnp.exp(scores - top), 0.0)
        total = jnp.sum(weight, axis=-1)
        rounded = weight.astype(jnp.bfloat16).astype(jnp.float32)
        numer = jnp.einsum('kgts,skd->kgtd', rounded, vblock)
        result = numer / total[..., None]
        return result.transpose(2, 0, 1, 3).reshape(block_rows, HQ * HEAD).astype(jnp.bfloat16)

    blocks = lax.map(one_block, jnp.arange(TOKENS // block_rows, dtype=jnp.int32))
    return blocks.reshape(TOKENS, HQ * HEAD)


def reference(queries, keys, values, doc_ids):
    attended = lax.map(attend_batch, (queries, keys, values, doc_ids))
    return jnp.roll(attended, 1, axis=0)
```

```python
import jax
import jax.numpy as jnp
from jax import lax
from jax.experimental import pallas as pl
from jax.experimental.pallas import tpu as pltpu
from jax.sharding import PartitionSpec as P

HQ = 32
HK = 4
HEAD = 128
GROUP = HQ // HK
BLOCK = 128
ROWS = BLOCK + 16
CHIPS = 32
WINDOW = 9
SCALE = 1.4426950408889634 / HEAD**0.5
FAR = -131072.0
NT = (((1,), (1,)), ((), ()))


def attend(chip, core, qs_ref, qf_ref, blocks, os_ref, of_ref, kaug, vaug):
    lane = lax.broadcasted_iota(jnp.int32, (BLOCK, HEAD), 1)
    row = lax.broadcasted_iota(jnp.int32, (BLOCK, HEAD), 0)
    below = jnp.zeros((1, HEAD), jnp.int32)
    ids = []
    for ref, back in blocks:
        for half in range(2):
            one = ref[half, BLOCK : BLOCK + 16, :HEAD][0:1].astype(jnp.float32)
            ids.append(jnp.where(chip >= back, one, -1.0))
    ids = jnp.concatenate(ids, axis=0)
    lane1 = lax.broadcasted_iota(jnp.int32, (1, HEAD), 1)
    for doc in range(1, 8):
        count = jnp.sum((ids < doc).astype(jnp.float32), axis=(0, 1), keepdims=True)
        below = jnp.where(lane1 == doc, count.astype(jnp.int32), below)
    ahead = jnp.sum((ids < 0).astype(jnp.float32), axis=(0, 1), keepdims=True).astype(jnp.int32)
    whole = 2 * WINDOW * BLOCK
    first = jnp.where(lane1 == 0, ahead, jnp.where(lane1 == 8, 0, jnp.where(lane1 > 8, whole, below)))
    last = pltpu.roll(below, HEAD - 1, 1)
    last = jnp.where(lane1 == 7, whole, jnp.where(lane1 == 8, ahead, jnp.where(lane1 > 8, whole, last)))
    one = jnp.ones((BLOCK, HEAD), jnp.bfloat16)
    for slot, (ref, back) in enumerate(blocks):
        for half in range(2):
            at = (2 * slot + half) * BLOCK
            place = (WINDOW - 1 - back) * 2 * BLOCK + (core ^ half) * BLOCK + row
            inside = (place >= first) & (place < last)
            hot = jnp.where(inside, 1.0, 0.0).astype(jnp.bfloat16)
            for kv in range(2):
                kaug[kv, at : at + BLOCK, :HEAD] = ref[half, :BLOCK, kv * HEAD : (kv + 1) * HEAD]
                kaug[kv, at : at + BLOCK, HEAD:] = hot
                vaug[kv, at : at + BLOCK, :HEAD] = ref[half, :BLOCK, (2 + kv) * HEAD : (3 + kv) * HEAD]
                vaug[kv, at : at + BLOCK, HEAD:] = one
    for q_ref, o_ref, half in ((qf_ref, of_ref, 1), (qs_ref, os_ref, 0)):
        place = (WINDOW - 1) * 2 * BLOCK + (core ^ half) * BLOCK + row
        inside = (place >= first) & (place < last)
        away = jnp.where(inside | (lane > 8), 0.0, FAR).astype(jnp.bfloat16)
        away = jnp.concatenate([away, away], axis=0)
        tall = lax.broadcasted_iota(jnp.int32, (2 * BLOCK, 2 * BLOCK), 0)
        wide = lax.broadcasted_iota(jnp.int32, (2 * BLOCK, 2 * BLOCK), 1)
        qat = (core ^ half) * BLOCK + (tall & (BLOCK - 1))
        kat = (core ^ (wide >> 7)) * BLOCK + (wide & (BLOCK - 1))
        future = kat > qat
        for kv in range(2):
            for pair in range(GROUP // 2):
                at = (kv * GROUP + 2 * pair) * HEAD
                q2 = jnp.concatenate([q_ref[:, at : at + HEAD], q_ref[:, at + HEAD : at + 2 * HEAD]], axis=0)
                q2 = jnp.concatenate([q2, away], axis=1)
                score = lax.dot_general(q2, kaug[kv], NT, preferred_element_type=jnp.float32)
                own = jnp.where(future, FAR, score[:, : 2 * BLOCK])
                score = jnp.concatenate([own, score[:, 2 * BLOCK :]], axis=1)
                top = jnp.max(score, axis=1, keepdims=True)
                weight = jnp.exp2((score - top) * SCALE).astype(jnp.bfloat16)
                both = jnp.dot(weight, vaug[kv], preferred_element_type=jnp.float32)
                result = (both[:, :HEAD] / both[:, HEAD:]).astype(jnp.bfloat16)
                o_ref[:, at : at + HEAD] = result[:BLOCK]
                o_ref[:, at + HEAD : at + 2 * HEAD] = result[BLOCK:]


def kernel(where_ref, qs, qf, b0, b4, b8, x1, x2, x3, os_ref, of_ref, kaug, vaug):
    chip, core = where_ref[0], where_ref[1]
    blocks = [(b0, 0), (b4, 4), (b8, 8)]
    for step, ref in ((1, x1), (2, x2), (3, x3)):
        blocks.append((ref.at[0], jnp.where(core == 0, step, 8 - step)))
        blocks.append((ref.at[1], jnp.where(core == 0, 4 + step, 4 - step)))
    attend(chip, core, qs, qf, blocks, os_ref, of_ref, kaug, vaug)


def attention(place, qs, qf, b0, b4, b8, x1, x2, x3):
    vmem = pl.BlockSpec(memory_space=pltpu.VMEM)
    keys = 2 * WINDOW * BLOCK
    rows = 2 * BLOCK * HQ // 2
    return pl.pallas_call(
        kernel,
        out_shape=[jax.ShapeDtypeStruct(qs.shape, jnp.bfloat16)] * 2,
        in_specs=[pl.BlockSpec(memory_space=pltpu.SMEM)] + [vmem] * 8,
        out_specs=[vmem] * 2,
        scratch_shapes=[pltpu.VMEM((2, keys, 2 * HEAD), jnp.bfloat16)] * 2,
        compiler_params=pltpu.CompilerParams(vmem_limit_bytes=48 * 1024 * 1024),
        cost_estimate=pl.CostEstimate(
            flops=8 * rows * keys * HEAD, bytes_accessed=6 << 20, transcendentals=rows * keys
        ),
    )(place, qs, qf, b0, b4, b8, x1, x2, x3)


def at(y, x, core):
    return ((y % 8) * 4 + x) * 2 + core


def shards(queries, keys, values, doc_ids):
    index = lax.axis_index("sp")
    chip, core = index // 2, index % 2
    first = core == 0

    def section(block, flip):
        pairs = [(p * 64 + s, (p + 1) % 8 * 64 + (s ^ flip)) for p in range(8) for s in range(64)]
        return lax.ppermute(block, ("pp", "sp"), pairs)

    def along_y(block):
        return lax.ppermute(block, "sp", [(s, (s + 8) % 64) for s in range(64)])

    def along_x(block):
        return lax.ppermute(block, "sp", [(s, (s + (2 if s % 2 == 0 else -2)) % 64) for s in range(64)])

    def swap(block):
        return lax.ppermute(block, "sp", [(s, s ^ 1) for s in range(64)])

    ids = jnp.pad(doc_ids[0].astype(jnp.bfloat16)[None], ((0, 15), (0, 384)))

    def part(j):
        cols = slice(j * 256, (j + 1) * 256)
        return jnp.concatenate([jnp.concatenate([keys[0][:, cols], values[0][:, cols]], axis=1), ids], axis=0)

    half0, half1 = part(0), part(1)
    same = section(jnp.where(first, half0, half1), 0)
    flip = section(jnp.where(first, half1, half0), 1)
    b0 = jnp.stack([same, flip])
    q = queries[0]
    qs = section(jnp.where(first, q[:, :2048], q[:, 2048:]), 0)
    qf = section(jnp.where(first, q[:, 2048:], q[:, :2048]), 1)
    b4 = along_y(b0)
    b8 = along_y(b4)
    x1 = along_x(jnp.stack([jnp.where(first, b0, b8), b4]))
    x2 = along_x(x1)
    x3 = along_x(x2)
    place = jnp.stack([chip, core]).astype(jnp.int32)
    os_, of_ = attention(place, qs, qf, b0, b4, b8, x1, x2, x3)
    got = swap(of_)
    out = jnp.where(first, jnp.concatenate([os_, got], axis=1), jnp.concatenate([got, os_], axis=1))
    return out[None]


def solution(mesh):
    return jax.shard_map(
        shards,
        mesh=mesh,
        in_specs=(P("pp", "sp", None), P("pp", "sp", None), P("pp", "sp", None), P("pp", "sp")),
        out_specs=P("pp", "sp", None),
        check_vma=False,
    )
```

```python
import functools

import jax
import jax.numpy as jnp
from jax import lax
from jax.experimental import pallas as pl
from jax.experimental.pallas import tpu as pltpu
from jax.sharding import PartitionSpec as P

HQ = 32
HK = 4
HEAD = 128
GROUP = HQ // HK
BLOCK = 128
ROWS = BLOCK + 16
SCALE = 1.4426950408889634 / HEAD**0.5
FAR = -131072.0
NT = (((1,), (1,)), ((), ()))


def marks(refs):
    ids = [ref[half, BLOCK : BLOCK + 16, :HEAD][0:1].astype(jnp.float32) for ref in refs for half in range(2)]
    ids = jnp.concatenate(ids, axis=0)
    lane = lax.broadcasted_iota(jnp.int32, ids.shape, 1)
    first = jnp.zeros(ids.shape, jnp.int32)
    last = jnp.zeros(ids.shape, jnp.int32)
    for doc in range(8):
        count = jnp.sum((ids <= doc).astype(jnp.float32), axis=1, keepdims=True).astype(jnp.int32)
        last = jnp.where(lane == doc, count, last)
        first = jnp.where(lane == doc + 1, count, first)
    first = jnp.where(lane > 7, BLOCK, first)
    return first, last


def piece(half, own, carried, last, n_blocks, core_ref, q_ref, *refs):
    b0 = refs[0]
    blocks = []
    for ref in refs[1 - own : n_blocks]:
        blocks.extend([ref] if len(ref.shape) == 3 else [ref.at[0], ref.at[1]])
    refs = refs[n_blocks:]
    old, refs = (refs[:3], refs[3:]) if carried else (None, refs)
    new, (kaug, vaug) = refs[:-2], refs[-2:]
    core = core_ref[0]
    row = lax.broadcasted_iota(jnp.int32, (BLOCK, HEAD), 0)
    lane = lax.broadcasted_iota(jnp.int32, (BLOCK, HEAD), 1)
    first, end = marks([b0] + blocks)
    one = jnp.ones((BLOCK, HEAD), jnp.bfloat16)
    for slot, ref in enumerate(blocks):
        for part in range(2):
            at = (2 * slot + part) * BLOCK
            mark = 2 * slot + part + 2
            inside = (row >= first[mark : mark + 1]) & (row < end[mark : mark + 1])
            hot = jnp.where(inside, 1.0, 0.0).astype(jnp.bfloat16)
            for kv in range(2):
                kaug[kv, at : at + BLOCK, :HEAD] = ref[part, :BLOCK, kv * HEAD : (kv + 1) * HEAD]
                kaug[kv, at : at + BLOCK, HEAD:] = hot
                vaug[kv, at : at + BLOCK, :HEAD] = ref[part, :BLOCK, (2 + kv) * HEAD : (3 + kv) * HEAD]
                vaug[kv, at : at + BLOCK, HEAD:] = one
    inside = (row >= first[half : half + 1]) & (row < end[half : half + 1])
    away = jnp.where(inside | (lane > 7), 0.0, FAR).astype(jnp.bfloat16)
    away = jnp.concatenate([away, away], axis=0)
    if own:
        tall = lax.broadcasted_iota(jnp.int32, (2 * BLOCK, 2 * BLOCK), 0)
        wide = lax.broadcasted_iota(jnp.int32, (2 * BLOCK, 2 * BLOCK), 1)
        qat = (core ^ half) * BLOCK + (tall & (BLOCK - 1))
        kat = (core ^ (wide >> 7)) * BLOCK + (wide & (BLOCK - 1))
        future = kat > qat
    for kv in range(2):
        for pair in range(GROUP // 2):
            head = kv * GROUP + 2 * pair
            at = head * HEAD
            rows = slice(head * BLOCK, (head + 2) * BLOCK)
            q2 = jnp.concatenate([q_ref[:, at : at + HEAD], q_ref[:, at + HEAD : at + 2 * HEAD]], axis=0)
            q2 = jnp.concatenate([q2, away], axis=1)
            score = lax.dot_general(q2, kaug[kv], NT, preferred_element_type=jnp.float32)
            if own:
                mine = jnp.where(future, FAR, score[:, : 2 * BLOCK])
                score = mine if len(blocks) == 1 else jnp.concatenate([mine, score[:, 2 * BLOCK :]], axis=1)
            top = jnp.max(score, axis=1, keepdims=True)
            if carried:
                before = old[0][rows, :]
                top = jnp.maximum(top, before[:, :1])
            weight = jnp.exp2((score - top) * SCALE).astype(jnp.bfloat16)
            both = jnp.dot(weight, vaug[kv], preferred_element_type=jnp.float32)
            total, accum = both[:, HEAD:], both[:, :HEAD]
            if carried:
                factor = jnp.exp2((before - top) * SCALE)
                total = total + old[1][rows, :] * factor
                accum = accum + old[2][rows, :] * factor
            if last:
                result = (accum / total).astype(jnp.bfloat16)
                new[0][:, at : at + HEAD] = result[:BLOCK]
                new[0][:, at + HEAD : at + 2 * HEAD] = result[BLOCK:]
            else:
                new[0][rows, :] = jnp.broadcast_to(top, (2 * BLOCK, HEAD))
                new[1][rows, :] = total
                new[2][rows, :] = accum


def attend(core, half, q, b0, blocks, own=False, state=(), last=False):
    vmem = pl.BlockSpec(memory_space=pltpu.VMEM)
    count = own + sum(1 if block.ndim == 3 else 2 for block in blocks)
    keys = 2 * BLOCK * count
    rows = BLOCK * HQ // 2
    if last:
        out_shape = jax.ShapeDtypeStruct(q.shape, jnp.bfloat16)
    else:
        out_shape = [jax.ShapeDtypeStruct((rows, HEAD), jnp.float32)] * 3
    return pl.pallas_call(
        functools.partial(piece, half, own, bool(state), last, 1 + len(blocks)),
        out_shape=out_shape,
        in_specs=[pl.BlockSpec(memory_space=pltpu.SMEM)] + [vmem] * (2 + len(blocks) + len(state)),
        out_specs=vmem if last else [vmem] * 3,
        scratch_shapes=[pltpu.VMEM((2, keys, 2 * HEAD), jnp.bfloat16)] * 2,
        compiler_params=pltpu.CompilerParams(vmem_limit_bytes=32 * 1024 * 1024),
        cost_estimate=pl.CostEstimate(
            flops=8 * rows * keys * HEAD, bytes_accessed=4 << 20, transcendentals=rows * keys
        ),
    )(core, q, b0, *blocks, *state)


def shards(queries, keys, values, doc_ids):
    core = lax.axis_index("sp") % 2
    first = core == 0

    def section(block, flip, dy=0):
        pairs = [(p * 64 + s, (p + 1) % 8 * 64 + ((s + 8 * dy) % 64 ^ flip)) for p in range(8) for s in range(64)]
        return lax.ppermute(block, ("pp", "sp"), pairs)

    def along_y(block):
        return lax.ppermute(block, "sp", [(s, (s + 8) % 64) for s in range(64)])

    def along_x(block, step0, step1):
        return lax.ppermute(block, "sp", [(s, (s + 2 * (step1 if s % 2 else step0)) % 64) for s in range(64)])

    def swap(block):
        return lax.ppermute(block, "sp", [(s, s ^ 1) for s in range(64)])

    ids = jnp.pad(doc_ids[0].astype(jnp.bfloat16)[None], ((0, 15), (0, 384)))

    def part(j):
        cols = slice(j * 256, (j + 1) * 256)
        return jnp.concatenate([jnp.concatenate([keys[0][:, cols], values[0][:, cols]], axis=1), ids], axis=0)

    half0, half1 = part(0), part(1)
    mine, other = jnp.where(first, half0, half1), jnp.where(first, half1, half0)
    q = queries[0]
    b0 = jnp.stack([section(mine, 0), section(other, 1)])
    b4 = jnp.stack([section(mine, 0, 1), section(other, 1, 1)])
    b0, b4, q = lax.optimization_barrier((b0, b4, q))
    qf = section(jnp.where(first, q[:, 2048:], q[:, :2048]), 1)
    b8 = along_y(b4)
    p1 = along_x(jnp.where(first, b0, b4), 1, -1)
    p2 = along_x(jnp.where(first, b4, b0), -1, 1)
    qf, b8, p1, p2, q, b0, b4 = lax.optimization_barrier((qf, b8, p1, p2, q, b0, b4))
    qs = section(jnp.where(first, q[:, :2048], q[:, 2048:]), 0)
    p3 = along_x(jnp.stack([jnp.where(first, b4, b8), p1]), 1, -1)
    p4 = along_x(jnp.where(first, b8, b4), -1, 1)
    place = core[None].astype(jnp.int32)
    state = attend(place, 1, qf, b0, [b4, b8, p1, p2], own=True)
    qs, p3, p4, qf, b0, b4, b8, p1, p2, *state = lax.optimization_barrier((qs, p3, p4, qf, b0, b4, b8, p1, p2, *state))
    p5 = along_x(p3[0], 1, -1)
    state2 = attend(place, 0, qs, b0, [b4, b8, p1, p2, p3, p4], own=True)
    p5, qs, qf, b0, p3, p4, *state2 = lax.optimization_barrier((p5, qs, qf, b0, p3, p4, *state2))
    of_ = attend(place, 1, qf, b0, [p3, p4, p5], state=state, last=True)
    got = swap(of_)
    os_ = attend(place, 0, qs, b0, [p5], state=state2, last=True)
    out = jnp.where(first, jnp.concatenate([os_, got], axis=1), jnp.concatenate([got, os_], axis=1))
    return out[None]


def solution(mesh):
    return jax.shard_map(
        shards,
        mesh=mesh,
        in_specs=(P("pp", "sp", None), P("pp", "sp", None), P("pp", "sp", None), P("pp", "sp")),
        out_specs=P("pp", "sp", None),
        check_vma=False,
    )
```

```python
import functools

import jax
import jax.numpy as jnp
from jax import lax
from jax.experimental import pallas as pl
from jax.experimental.pallas import tpu as pltpu
from jax.sharding import PartitionSpec as P

HQ = 32
HK = 4
HEAD = 128
GROUP = HQ // HK
BLOCK = 128
ROWS = BLOCK + 16
SCALE = 1.4426950408889634 / HEAD**0.5
FAR = -131072.0
NT = (((1,), (1,)), ((), ()))


def marks(refs):
    ids = [ref[half, BLOCK : BLOCK + 16, :HEAD][0:1].astype(jnp.float32) for ref in refs for half in range(2)]
    ids = jnp.concatenate(ids, axis=0)
    lane = lax.broadcasted_iota(jnp.int32, ids.shape, 1)
    first = jnp.zeros(ids.shape, jnp.int32)
    last = jnp.zeros(ids.shape, jnp.int32)
    for doc in range(8):
        count = jnp.sum((ids <= doc).astype(jnp.float32), axis=1, keepdims=True).astype(jnp.int32)
        last = jnp.where(lane == doc, count, last)
        first = jnp.where(lane == doc + 1, count, first)
    first = jnp.where(lane > 7, BLOCK, first)
    return first, last


def piece(half, own, carried, last, n_blocks, core_ref, q_ref, *refs):
    b0 = refs[0]
    blocks = []
    for ref in refs[1 - own : n_blocks]:
        blocks.extend([ref] if len(ref.shape) == 3 else [ref.at[0], ref.at[1]])
    refs = refs[n_blocks:]
    old, refs = (refs[:3], refs[3:]) if carried else (None, refs)
    new, (kaug, vaug) = refs[:-2], refs[-2:]
    core = core_ref[0]
    row = lax.broadcasted_iota(jnp.int32, (BLOCK, HEAD), 0)
    lane = lax.broadcasted_iota(jnp.int32, (BLOCK, HEAD), 1)
    first, end = marks([b0] + blocks)
    one = jnp.ones((BLOCK, HEAD), jnp.bfloat16)
    for slot, ref in enumerate(blocks):
        for part in range(2):
            at = (2 * slot + part) * BLOCK
            mark = 2 * slot + part + 2
            inside = (row >= first[mark : mark + 1]) & (row < end[mark : mark + 1])
            hot = jnp.where(inside, 1.0, 0.0).astype(jnp.bfloat16)
            for kv in range(2):
                kaug[kv, at : at + BLOCK, :HEAD] = ref[part, :BLOCK, kv * HEAD : (kv + 1) * HEAD]
                kaug[kv, at : at + BLOCK, HEAD:] = hot
                vaug[kv, at : at + BLOCK, :HEAD] = ref[part, :BLOCK, (2 + kv) * HEAD : (3 + kv) * HEAD]
                vaug[kv, at : at + BLOCK, HEAD:] = one
    inside = (row >= first[half : half + 1]) & (row < end[half : half + 1])
    away = jnp.where(inside | (lane > 7), 0.0, FAR).astype(jnp.bfloat16)
    away = jnp.concatenate([away, away], axis=0)
    if own:
        tall = lax.broadcasted_iota(jnp.int32, (2 * BLOCK, 2 * BLOCK), 0)
        wide = lax.broadcasted_iota(jnp.int32, (2 * BLOCK, 2 * BLOCK), 1)
        qat = (core ^ half) * BLOCK + (tall & (BLOCK - 1))
        kat = (core ^ (wide >> 7)) * BLOCK + (wide & (BLOCK - 1))
        future = kat > qat
    for kv in range(2):
        for pair in range(GROUP // 2):
            head = kv * GROUP + 2 * pair
            at = head * HEAD
            rows = slice(head * BLOCK, (head + 2) * BLOCK)
            q2 = jnp.concatenate([q_ref[:, at : at + HEAD], q_ref[:, at + HEAD : at + 2 * HEAD]], axis=0)
            q2 = jnp.concatenate([q2, away], axis=1)
            score = lax.dot_general(q2, kaug[kv], NT, preferred_element_type=jnp.float32)
            if own:
                mine = jnp.where(future, FAR, score[:, : 2 * BLOCK])
                score = mine if len(blocks) == 1 else jnp.concatenate([mine, score[:, 2 * BLOCK :]], axis=1)
            top = jnp.max(score, axis=1, keepdims=True)
            if carried:
                before = old[0][rows, :]
                top = jnp.maximum(jnp.broadcast_to(top, before.shape), before)
            wide = jnp.concatenate([top] * (2 * len(blocks)), axis=1) if carried else top
            weight = jnp.exp2((score - wide) * SCALE).astype(jnp.bfloat16)
            both = jnp.dot(weight, vaug[kv], preferred_element_type=jnp.float32)
            total, accum = both[:, HEAD:], both[:, :HEAD]
            if carried:
                factor = jnp.exp2((before - top) * SCALE)
                total = total + old[1][rows, :] * factor
                accum = accum + old[2][rows, :] * factor
            if last:
                result = (accum / total).astype(jnp.bfloat16)
                new[0][:, at : at + HEAD] = result[:BLOCK]
                new[0][:, at + HEAD : at + 2 * HEAD] = result[BLOCK:]
            else:
                new[0][rows, :] = jnp.broadcast_to(top, (2 * BLOCK, HEAD))
                new[1][rows, :] = total
                new[2][rows, :] = accum


def attend(core, half, q, b0, blocks, own=False, state=(), last=False):
    vmem = pl.BlockSpec(memory_space=pltpu.VMEM)
    count = own + sum(1 if block.ndim == 3 else 2 for block in blocks)
    keys = 2 * BLOCK * count
    rows = BLOCK * HQ // 2
    if last:
        out_shape = jax.ShapeDtypeStruct(q.shape, jnp.bfloat16)
    else:
        out_shape = [jax.ShapeDtypeStruct((rows, HEAD), jnp.float32)] * 3
    return pl.pallas_call(
        functools.partial(piece, half, own, bool(state), last, 1 + len(blocks)),
        out_shape=out_shape,
        in_specs=[pl.BlockSpec(memory_space=pltpu.SMEM)] + [vmem] * (2 + len(blocks) + len(state)),
        out_specs=vmem if last else [vmem] * 3,
        scratch_shapes=[pltpu.VMEM((2, keys, 2 * HEAD), jnp.bfloat16)] * 2,
        compiler_params=pltpu.CompilerParams(vmem_limit_bytes=32 * 1024 * 1024),
        cost_estimate=pl.CostEstimate(
            flops=8 * rows * keys * HEAD, bytes_accessed=4 << 20, transcendentals=rows * keys
        ),
    )(core, q, b0, *blocks, *state)


def shards(queries, keys, values, doc_ids):
    core = lax.axis_index("sp") % 2
    first = core == 0

    def section(block, flip, dy=0):
        pairs = [(p * 64 + s, (p + 1) % 8 * 64 + ((s + 8 * dy) % 64 ^ flip)) for p in range(8) for s in range(64)]
        return lax.ppermute(block, ("pp", "sp"), pairs)

    def along_y(block):
        return lax.ppermute(block, "sp", [(s, (s + 8) % 64) for s in range(64)])

    def along_x(block, step0, step1):
        return lax.ppermute(block, "sp", [(s, (s + 2 * (step1 if s % 2 else step0)) % 64) for s in range(64)])

    def swap(block):
        return lax.ppermute(block, "sp", [(s, s ^ 1) for s in range(64)])

    ids = jnp.pad(doc_ids[0].astype(jnp.bfloat16)[None], ((0, 15), (0, 384)))

    def part(j):
        cols = slice(j * 256, (j + 1) * 256)
        return jnp.concatenate([jnp.concatenate([keys[0][:, cols], values[0][:, cols]], axis=1), ids], axis=0)

    half0, half1 = part(0), part(1)
    mine, other = jnp.where(first, half0, half1), jnp.where(first, half1, half0)
    q = queries[0]
    b0 = jnp.stack([section(mine, 0), section(other, 1)])
    b4 = jnp.stack([section(mine, 0, 1), section(other, 1, 1)])
    b0, b4, q = lax.optimization_barrier((b0, b4, q))
    qf = section(jnp.where(first, q[:, 2048:], q[:, :2048]), 1)
    b8 = along_y(b4)
    p1 = along_x(jnp.where(first, b0, b4), 1, -1)
    p2 = along_x(jnp.where(first, b4, b0), -1, 1)
    b8, qf = lax.optimization_barrier((b8, qf))
    qf, b8, p1, p2, q, b0, b4 = lax.optimization_barrier((qf, b8, p1, p2, q, b0, b4))
    qs = section(jnp.where(first, q[:, :2048], q[:, 2048:]), 0)
    p3 = along_x(jnp.stack([jnp.where(first, b4, b8), p1]), 1, -1)
    p4 = along_y(p2)
    place = core[None].astype(jnp.int32)
    state = attend(place, 1, qf, b0, [b4, b8, p1, p2], own=True)
    qs, qf = lax.optimization_barrier((qs, qf))
    qs, p3, p4, qf, b0, b4, b8, p1, p2, *state = lax.optimization_barrier((qs, p3, p4, qf, b0, b4, b8, p1, p2, *state))
    p5 = along_x(p3[0], 1, -1)
    state2 = attend(place, 0, qs, b0, [b4, b8, p1, p2, p3, p4], own=True)
    p5, qs, qf, b0, p3, p4, *state2 = lax.optimization_barrier((p5, qs, qf, b0, p3, p4, *state2))
    of_ = attend(place, 1, qf, b0, [p3, p4, p5], state=state, last=True)
    got = swap(of_)
    os_ = attend(place, 0, qs, b0, [p5], state=state2, last=True)
    out = jnp.where(first, jnp.concatenate([os_, got], axis=1), jnp.concatenate([got, os_], axis=1))
    return out[None]


def solution(mesh):
    return jax.shard_map(
        shards,
        mesh=mesh,
        in_specs=(P("pp", "sp", None), P("pp", "sp", None), P("pp", "sp", None), P("pp", "sp")),
        out_specs=P("pp", "sp", None),
        check_vma=False,
    )
```

```python
import functools

import jax
import jax.numpy as jnp
from jax import lax
from jax.experimental import pallas as pl
from jax.experimental.pallas import tpu as pltpu
from jax.sharding import PartitionSpec as P

HQ = 32
HK = 4
HEAD = 128
GROUP = HQ // HK
BLOCK = 128
ROWS = BLOCK + 16
SCALE = 1.4426950408889634 / HEAD**0.5
FAR = -131072.0
NT = (((1,), (1,)), ((), ()))


def marks(refs):
    ids = [ref[half, BLOCK : BLOCK + 16, :HEAD][0:1].astype(jnp.float32) for ref in refs for half in range(2)]
    ids = jnp.concatenate(ids, axis=0)
    lane = lax.broadcasted_iota(jnp.int32, ids.shape, 1)
    first = jnp.zeros(ids.shape, jnp.int32)
    last = jnp.zeros(ids.shape, jnp.int32)
    for doc in range(8):
        count = jnp.sum((ids <= doc).astype(jnp.float32), axis=1, keepdims=True).astype(jnp.int32)
        last = jnp.where(lane == doc, count, last)
        first = jnp.where(lane == doc + 1, count, first)
    first = jnp.where(lane > 7, BLOCK, first)
    return first, last


def piece(half, own, carried, last, n_blocks, core_ref, q_ref, *refs):
    b0 = refs[0]
    blocks = []
    for ref in refs[1 - own : n_blocks]:
        blocks.extend([ref] if len(ref.shape) == 3 else [ref.at[0], ref.at[1]])
    refs = refs[n_blocks:]
    old, refs = (refs[:3], refs[3:]) if carried else (None, refs)
    new, (kaug, vaug) = refs[:-2], refs[-2:]
    core = core_ref[0]
    row = lax.broadcasted_iota(jnp.int32, (BLOCK, HEAD), 0)
    lane = lax.broadcasted_iota(jnp.int32, (BLOCK, HEAD), 1)
    first, end = marks([b0] + blocks)
    one = jnp.ones((BLOCK, HEAD), jnp.bfloat16)
    for slot, ref in enumerate(blocks):
        for part in range(2):
            at = (2 * slot + part) * BLOCK
            mark = 2 * slot + part + 2
            inside = (row >= first[mark : mark + 1]) & (row < end[mark : mark + 1])
            hot = jnp.where(inside, 1.0, 0.0).astype(jnp.bfloat16)
            for kv in range(2):
                kaug[kv, at : at + BLOCK, :HEAD] = ref[part, :BLOCK, kv * HEAD : (kv + 1) * HEAD]
                kaug[kv, at : at + BLOCK, HEAD:] = hot
                vaug[kv, at : at + BLOCK, :HEAD] = ref[part, :BLOCK, (2 + kv) * HEAD : (3 + kv) * HEAD]
                vaug[kv, at : at + BLOCK, HEAD:] = one
    inside = (row >= first[half : half + 1]) & (row < end[half : half + 1])
    away = jnp.where(inside | (lane > 7), 0.0, FAR).astype(jnp.bfloat16)
    away = jnp.concatenate([away, away], axis=0)
    if own:
        tall = lax.broadcasted_iota(jnp.int32, (2 * BLOCK, 2 * BLOCK), 0)
        wide = lax.broadcasted_iota(jnp.int32, (2 * BLOCK, 2 * BLOCK), 1)
        qat = (core ^ half) * BLOCK + (tall & (BLOCK - 1))
        kat = (core ^ (wide >> 7)) * BLOCK + (wide & (BLOCK - 1))
        future = kat > qat
    for kv in range(2):
        for pair in range(GROUP // 2):
            head = kv * GROUP + 2 * pair
            at = head * HEAD
            rows = slice(head * BLOCK, (head + 2) * BLOCK)
            q2 = jnp.concatenate([q_ref[:, at : at + HEAD], q_ref[:, at + HEAD : at + 2 * HEAD]], axis=0)
            q2 = jnp.concatenate([q2, away], axis=1)
            score = lax.dot_general(q2, kaug[kv], NT, preferred_element_type=jnp.float32)
            if own:
                mine = jnp.where(future, FAR, score[:, : 2 * BLOCK])
                score = mine if len(blocks) == 1 else jnp.concatenate([mine, score[:, 2 * BLOCK :]], axis=1)
            top = jnp.max(score, axis=1, keepdims=True)
            if carried:
                before = old[0][rows, :]
                top = jnp.maximum(jnp.broadcast_to(top, before.shape), before)
            wide = jnp.concatenate([top] * (2 * len(blocks)), axis=1) if carried else top
            weight = jnp.exp2((score - wide) * SCALE).astype(jnp.bfloat16)
            both = jnp.dot(weight, vaug[kv], preferred_element_type=jnp.float32)
            total, accum = both[:, HEAD:], both[:, :HEAD]
            if carried:
                factor = jnp.exp2((before - top) * SCALE)
                total = total + old[1][rows, :] * factor
                accum = accum + old[2][rows, :] * factor
            if last:
                result = (accum / total).astype(jnp.bfloat16)
                new[0][:, at : at + HEAD] = result[:BLOCK]
                new[0][:, at + HEAD : at + 2 * HEAD] = result[BLOCK:]
            else:
                new[0][rows, :] = jnp.broadcast_to(top, (2 * BLOCK, HEAD))
                new[1][rows, :] = total
                new[2][rows, :] = accum


def attend(core, half, q, b0, blocks, own=False, state=(), last=False):
    vmem = pl.BlockSpec(memory_space=pltpu.VMEM)
    count = own + sum(1 if block.ndim == 3 else 2 for block in blocks)
    keys = 2 * BLOCK * count
    rows = BLOCK * HQ // 2
    if last:
        out_shape = jax.ShapeDtypeStruct(q.shape, jnp.bfloat16)
    else:
        out_shape = [jax.ShapeDtypeStruct((rows, HEAD), jnp.float32)] * 3
    return pl.pallas_call(
        functools.partial(piece, half, own, bool(state), last, 1 + len(blocks)),
        out_shape=out_shape,
        in_specs=[pl.BlockSpec(memory_space=pltpu.SMEM)] + [vmem] * (2 + len(blocks) + len(state)),
        out_specs=vmem if last else [vmem] * 3,
        scratch_shapes=[pltpu.VMEM((2, keys, 2 * HEAD), jnp.bfloat16)] * 2,
        compiler_params=pltpu.CompilerParams(vmem_limit_bytes=32 * 1024 * 1024),
        cost_estimate=pl.CostEstimate(
            flops=8 * rows * keys * HEAD, bytes_accessed=4 << 20, transcendentals=rows * keys
        ),
    )(core, q, b0, *blocks, *state)


def shards(queries, keys, values, doc_ids):
    place = lax.axis_index("sp")
    core, column = place % 2, place // 2 % 4
    first = core == 0

    def section(block, flip, dy=0):
        pairs = [(p * 64 + s, (p + 1) % 8 * 64 + ((s + 8 * dy) % 64 ^ flip)) for p in range(8) for s in range(64)]
        return lax.ppermute(block, ("pp", "sp"), pairs)

    def along_y(block):
        return lax.ppermute(block, "sp", [(s, (s + 8) % 64) for s in range(64)])

    def even_pair(block):
        return lax.ppermute(block, "sp", [(s, s ^ 2) for s in range(64)])

    def odd_pair(block):
        return lax.ppermute(block, "sp", [(s, s // 8 * 8 + (s + (2 if s & 2 else -2)) % 8) for s in range(64)])

    def swap(block):
        return lax.ppermute(block, "sp", [(s, s ^ 1) for s in range(64)])

    ids = jnp.pad(doc_ids[0].astype(jnp.bfloat16)[None], ((0, 15), (0, 384)))

    def part(j):
        cols = slice(j * 256, (j + 1) * 256)
        return jnp.concatenate([jnp.concatenate([keys[0][:, cols], values[0][:, cols]], axis=1), ids], axis=0)

    half0, half1 = part(0), part(1)
    mine, other = jnp.where(first, half0, half1), jnp.where(first, half1, half0)
    q = queries[0]
    b4 = jnp.stack([section(mine, 0, 1), section(other, 1, 1)])
    b4, q = lax.optimization_barrier((b4, q))
    b8 = along_y(b4)
    e1 = even_pair(b4)
    f1 = odd_pair(b4)
    b0 = jnp.stack(lax.optimization_barrier((section(mine, 0), section(other, 1))))
    qf = section(jnp.where(first, q[:, 2048:], q[:, :2048]), 1)
    b8, e1, f1, b0, b4 = lax.optimization_barrier((b8, e1, f1, b0, b4))
    qs = section(jnp.where(first, q[:, :2048], q[:, 2048:]), 0)
    f2 = odd_pair(jnp.where(column < 2, b0, b8))
    e2 = even_pair(jnp.where(column % 2 == 0, b0, b8))
    at = core[None].astype(jnp.int32)
    state = attend(at, 1, qf, b0, [b4, b8, e1, f1], own=True)
    e2, f2, qf, b0, b4, b8, e1, f1, *state = lax.optimization_barrier((e2, f2, qf, b0, b4, b8, e1, f1, *state))
    e3 = even_pair(f2)
    f3 = odd_pair(e1)
    state2 = attend(at, 0, qs, b0, [b4, b8, e1, f1, e2, f2], own=True)
    e3, f3, qs, qf, b0, e2, f2, *state2 = lax.optimization_barrier((e3, f3, qs, qf, b0, e2, f2, *state2))
    of_ = attend(at, 1, qf, b0, [e2, f2, e3, f3], state=state, last=True)
    got = swap(of_)
    os_ = attend(at, 0, qs, b0, [e3, f3], state=state2, last=True)
    out = jnp.where(first, jnp.concatenate([os_, got], axis=1), jnp.concatenate([got, os_], axis=1))
    return out[None]


def solution(mesh):
    return jax.shard_map(
        shards,
        mesh=mesh,
        in_specs=(P("pp", "sp", None), P("pp", "sp", None), P("pp", "sp", None), P("pp", "sp")),
        out_specs=P("pp", "sp", None),
        check_vma=False,
    )
```

```python
import functools

import jax
import jax.numpy as jnp
from jax import lax
from jax.experimental import pallas as pl
from jax.experimental.pallas import tpu as pltpu
from jax.sharding import PartitionSpec as P

HQ = 32
HK = 4
HEAD = 128
GROUP = HQ // HK
BLOCK = 128
ROWS = BLOCK + 16
SCALE = 1.4426950408889634 / HEAD**0.5
FAR = -131072.0
NT = (((1,), (1,)), ((), ()))


def marks(refs):
    ids = [ref[half, BLOCK : BLOCK + 16, :HEAD][0:1].astype(jnp.float32) for ref in refs for half in range(2)]
    ids = jnp.concatenate(ids, axis=0)
    lane = lax.broadcasted_iota(jnp.int32, ids.shape, 1)
    first = jnp.zeros(ids.shape, jnp.int32)
    last = jnp.zeros(ids.shape, jnp.int32)
    for doc in range(8):
        count = jnp.sum((ids <= doc).astype(jnp.float32), axis=1, keepdims=True).astype(jnp.int32)
        last = jnp.where(lane == doc, count, last)
        first = jnp.where(lane == doc + 1, count, first)
    first = jnp.where(lane > 7, BLOCK, first)
    return first, last


def piece(half, own, carried, last, n_blocks, core_ref, q_ref, *refs):
    b0 = refs[0]
    blocks = []
    for ref in refs[1 - own : n_blocks]:
        blocks.extend([ref] if len(ref.shape) == 3 else [ref.at[0], ref.at[1]])
    refs = refs[n_blocks:]
    old, refs = (refs[:3], refs[3:]) if carried else (None, refs)
    new, (kaug, vaug) = refs[:-2], refs[-2:]
    core = core_ref[0]
    row = lax.broadcasted_iota(jnp.int32, (BLOCK, HEAD), 0)
    lane = lax.broadcasted_iota(jnp.int32, (BLOCK, HEAD), 1)
    first, end = marks([b0] + blocks)
    one = jnp.ones((BLOCK, HEAD), jnp.bfloat16)
    for slot, ref in enumerate(blocks):
        for part in range(2):
            at = (2 * slot + part) * BLOCK
            mark = 2 * slot + part + 2
            inside = (row >= first[mark : mark + 1]) & (row < end[mark : mark + 1])
            hot = jnp.where(inside, 1.0, 0.0).astype(jnp.bfloat16)
            for kv in range(2):
                kaug[kv, at : at + BLOCK, :HEAD] = ref[part, :BLOCK, kv * HEAD : (kv + 1) * HEAD]
                kaug[kv, at : at + BLOCK, HEAD:] = hot
                vaug[kv, at : at + BLOCK, :HEAD] = ref[part, :BLOCK, (2 + kv) * HEAD : (3 + kv) * HEAD]
                vaug[kv, at : at + BLOCK, HEAD:] = one
    inside = (row >= first[half : half + 1]) & (row < end[half : half + 1])
    away = jnp.where(inside | (lane > 7), 0.0, FAR).astype(jnp.bfloat16)
    away = jnp.concatenate([away, away], axis=0)
    if own:
        tall = lax.broadcasted_iota(jnp.int32, (2 * BLOCK, 2 * BLOCK), 0)
        wide = lax.broadcasted_iota(jnp.int32, (2 * BLOCK, 2 * BLOCK), 1)
        qat = (core ^ half) * BLOCK + (tall & (BLOCK - 1))
        kat = (core ^ (wide >> 7)) * BLOCK + (wide & (BLOCK - 1))
        future = kat > qat
    for kv in range(2):
        for pair in range(GROUP // 2):
            head = kv * GROUP + 2 * pair
            at = head * HEAD
            rows = slice(head * BLOCK, (head + 2) * BLOCK)
            q2 = jnp.concatenate([q_ref[:, at : at + HEAD], q_ref[:, at + HEAD : at + 2 * HEAD]], axis=0)
            q2 = jnp.concatenate([q2, away], axis=1)
            score = lax.dot_general(q2, kaug[kv], NT, preferred_element_type=jnp.float32)
            if own:
                mine = jnp.where(future, FAR, score[:, : 2 * BLOCK])
                score = mine if len(blocks) == 1 else jnp.concatenate([mine, score[:, 2 * BLOCK :]], axis=1)
            top = jnp.max(score, axis=1, keepdims=True)
            if carried:
                before = old[0][rows, :]
                top = jnp.maximum(jnp.broadcast_to(top, before.shape), before)
            wide = jnp.concatenate([top] * (2 * len(blocks)), axis=1) if carried else top
            weight = jnp.exp2((score - wide) * SCALE).astype(jnp.bfloat16)
            both = jnp.dot(weight, vaug[kv], preferred_element_type=jnp.float32)
            total, accum = both[:, HEAD:], both[:, :HEAD]
            if carried:
                factor = jnp.exp2((before - top) * SCALE)
                total = total + old[1][rows, :] * factor
                accum = accum + old[2][rows, :] * factor
            if last:
                result = (accum / total).astype(jnp.bfloat16)
                new[0][:, at : at + HEAD] = result[:BLOCK]
                new[0][:, at + HEAD : at + 2 * HEAD] = result[BLOCK:]
            else:
                new[0][rows, :] = jnp.broadcast_to(top, (2 * BLOCK, HEAD))
                new[1][rows, :] = total
                new[2][rows, :] = accum


def attend(core, half, q, b0, blocks, own=False, state=(), last=False):
    vmem = pl.BlockSpec(memory_space=pltpu.VMEM)
    count = own + sum(1 if block.ndim == 3 else 2 for block in blocks)
    keys = 2 * BLOCK * count
    rows = BLOCK * HQ // 2
    if last:
        out_shape = jax.ShapeDtypeStruct(q.shape, jnp.bfloat16)
    else:
        out_shape = [jax.ShapeDtypeStruct((rows, HEAD), jnp.float32)] * 3
    return pl.pallas_call(
        functools.partial(piece, half, own, bool(state), last, 1 + len(blocks)),
        out_shape=out_shape,
        in_specs=[pl.BlockSpec(memory_space=pltpu.SMEM)] + [vmem] * (2 + len(blocks) + len(state)),
        out_specs=vmem if last else [vmem] * 3,
        scratch_shapes=[pltpu.VMEM((2, keys, 2 * HEAD), jnp.bfloat16)] * 2,
        compiler_params=pltpu.CompilerParams(vmem_limit_bytes=32 * 1024 * 1024),
        cost_estimate=pl.CostEstimate(
            flops=8 * rows * keys * HEAD, bytes_accessed=4 << 20, transcendentals=rows * keys
        ),
    )(core, q, b0, *blocks, *state)


def shards(queries, keys, values, doc_ids):
    place = lax.axis_index("sp")
    core, column = place % 2, place // 2 % 4
    first = core == 0

    def section(block, flip, dy=0):
        pairs = [(p * 64 + s, (p + 1) % 8 * 64 + ((s + 8 * dy) % 64 ^ flip)) for p in range(8) for s in range(64)]
        return lax.ppermute(block, ("pp", "sp"), pairs)

    def along_y(block, step0, step1):
        return lax.ppermute(block, "sp", [(s, (s + 8 * (step1 if s % 2 else step0)) % 64) for s in range(64)])

    def even_pair(block):
        return lax.ppermute(block, "sp", [(s, s ^ 2) for s in range(64)])

    def odd_pair(block):
        return lax.ppermute(block, "sp", [(s, s // 8 * 8 + (s + (2 if s & 2 else -2)) % 8) for s in range(64)])

    def swap(block):
        return lax.ppermute(block, "sp", [(s, s ^ 1) for s in range(64)])

    ids = jnp.pad(doc_ids[0].astype(jnp.bfloat16)[None], ((0, 15), (0, 384)))

    def part(j):
        cols = slice(j * 256, (j + 1) * 256)
        return jnp.concatenate([jnp.concatenate([keys[0][:, cols], values[0][:, cols]], axis=1), ids], axis=0)

    half0, half1 = part(0), part(1)
    mine, other = jnp.where(first, half0, half1), jnp.where(first, half1, half0)
    q = queries[0]
    b4 = jnp.stack([section(mine, 0, 1), section(other, 1, 1)])
    qf = section(jnp.where(first, q[:, 2048:], q[:, :2048]), 1)
    qs = section(jnp.where(first, q[:, :2048], q[:, 2048:]), 0)
    (b4,) = lax.optimization_barrier((b4,))
    ya = along_y(b4, 1, -1)
    yb = along_y(b4, -1, 1)
    e1 = even_pair(b4)
    ya, yb, b4, qf = lax.optimization_barrier((ya, yb, b4, qf))
    f2 = odd_pair(jnp.where((column < 2) == first, yb, ya))
    e2 = even_pair(jnp.where((column % 2 == 0) == first, yb, ya))
    f1 = odd_pair(b4)
    b0, b8 = jnp.where(first, yb, ya), jnp.where(first, ya, yb)
    at = core[None].astype(jnp.int32)
    state = attend(at, 1, qf, b0, [b4, b8, e1], own=True)
    f2, e1, *state = lax.optimization_barrier((f2, e1, *state))
    f3 = odd_pair(e1)
    e3 = even_pair(f2)
    state2 = attend(at, 0, qs, b0, [b4, b8, e1, f1, e2, f2], own=True)
    state = attend(at, 1, qf, b0, [f1, e2, f2], state=state)
    e3, f3, qs, qf, b0, *both = lax.optimization_barrier((e3, f3, qs, qf, b0, *state, *state2))
    of_ = attend(at, 1, qf, b0, [e3, f3], state=both[:3], last=True)
    got = swap(of_)
    os_ = attend(at, 0, qs, b0, [e3, f3], state=both[3:], last=True)
    out = jnp.where(first, jnp.concatenate([os_, got], axis=1), jnp.concatenate([got, os_], axis=1))
    return out[None]


def solution(mesh):
    return jax.shard_map(
        shards,
        mesh=mesh,
        in_specs=(P("pp", "sp", None), P("pp", "sp", None), P("pp", "sp", None), P("pp", "sp")),
        out_specs=P("pp", "sp", None),
        check_vma=False,
    )
```

```python
import functools

import jax
import jax.numpy as jnp
from jax import lax
from jax.experimental import pallas as pl
from jax.experimental.pallas import tpu as pltpu
from jax.sharding import PartitionSpec as P

HQ = 32
HK = 4
HEAD = 128
GROUP = HQ // HK
BLOCK = 128
ROWS = BLOCK + 16
SCALE = 1.4426950408889634 / HEAD**0.5
FAR = -131072.0
NT = (((1,), (1,)), ((), ()))


def marks(refs):
    ids = [ref[half, BLOCK : BLOCK + 16, :HEAD][0:1].astype(jnp.float32) for ref in refs for half in range(2)]
    ids = jnp.concatenate(ids, axis=0)
    lane = lax.broadcasted_iota(jnp.int32, ids.shape, 1)
    first = jnp.zeros(ids.shape, jnp.int32)
    last = jnp.zeros(ids.shape, jnp.int32)
    for doc in range(8):
        count = jnp.sum((ids <= doc).astype(jnp.float32), axis=1, keepdims=True).astype(jnp.int32)
        last = jnp.where(lane == doc, count, last)
        first = jnp.where(lane == doc + 1, count, first)
    first = jnp.where(lane > 7, BLOCK, first)
    return first, last


def piece(half, own, carried, last, n_blocks, core_ref, q_ref, *refs):
    b0 = refs[0]
    blocks = []
    for ref in refs[1 - own : n_blocks]:
        blocks.extend([ref] if len(ref.shape) == 3 else [ref.at[0], ref.at[1]])
    refs = refs[n_blocks:]
    old, refs = (refs[:3], refs[3:]) if carried else (None, refs)
    new, (kaug, vaug) = refs[:-2], refs[-2:]
    core = core_ref[0]
    row = lax.broadcasted_iota(jnp.int32, (BLOCK, HEAD), 0)
    lane = lax.broadcasted_iota(jnp.int32, (BLOCK, HEAD), 1)
    first, end = marks([b0] + blocks)
    one = jnp.ones((BLOCK, HEAD), jnp.bfloat16)
    for slot, ref in enumerate(blocks):
        for part in range(2):
            at = (2 * slot + part) * BLOCK
            mark = 2 * slot + part + 2
            inside = (row >= first[mark : mark + 1]) & (row < end[mark : mark + 1])
            hot = jnp.where(inside, 1.0, 0.0).astype(jnp.bfloat16)
            for kv in range(2):
                kaug[kv, at : at + BLOCK, :HEAD] = ref[part, :BLOCK, kv * HEAD : (kv + 1) * HEAD]
                kaug[kv, at : at + BLOCK, HEAD:] = hot
                vaug[kv, at : at + BLOCK, :HEAD] = ref[part, :BLOCK, (2 + kv) * HEAD : (3 + kv) * HEAD]
                vaug[kv, at : at + BLOCK, HEAD:] = one
    inside = (row >= first[half : half + 1]) & (row < end[half : half + 1])
    away = jnp.where(inside | (lane > 7), 0.0, FAR).astype(jnp.bfloat16)
    away = jnp.concatenate([away, away], axis=0)
    if own:
        tall = lax.broadcasted_iota(jnp.int32, (2 * BLOCK, 2 * BLOCK), 0)
        wide = lax.broadcasted_iota(jnp.int32, (2 * BLOCK, 2 * BLOCK), 1)
        qat = (core ^ half) * BLOCK + (tall & (BLOCK - 1))
        kat = (core ^ (wide >> 7)) * BLOCK + (wide & (BLOCK - 1))
        future = kat > qat
    def scores(kv, pair):
        at = (kv * GROUP + 2 * pair) * HEAD
        q2 = jnp.concatenate([q_ref[:, at : at + HEAD], q_ref[:, at + HEAD : at + 2 * HEAD]], axis=0)
        q2 = jnp.concatenate([q2, away], axis=1)
        score = lax.dot_general(q2, kaug[kv], NT, preferred_element_type=jnp.float32)
        if own:
            mine = jnp.where(future, FAR, score[:, : 2 * BLOCK])
            score = mine if len(blocks) == 1 else jnp.concatenate([mine, score[:, 2 * BLOCK :]], axis=1)
        return score

    def weights(score, kv, pair):
        head = kv * GROUP + 2 * pair
        rows = slice(head * BLOCK, (head + 2) * BLOCK)
        top = jnp.max(score, axis=1, keepdims=True)
        factor = None
        if carried:
            before = old[0][rows, :]
            top = jnp.maximum(jnp.broadcast_to(top, before.shape), before)
            factor = jnp.exp2((before - top) * SCALE)
        wide = jnp.concatenate([top] * (2 * len(blocks)), axis=1) if carried else top
        return jnp.exp2((score - wide) * SCALE).astype(jnp.bfloat16), top, factor

    def finish(weight, top, factor, kv, pair):
        head = kv * GROUP + 2 * pair
        at = head * HEAD
        rows = slice(head * BLOCK, (head + 2) * BLOCK)
        both = jnp.dot(weight, vaug[kv], preferred_element_type=jnp.float32)
        total, accum = both[:, HEAD:], both[:, :HEAD]
        if carried:
            total = total + old[1][rows, :] * factor
            accum = accum + old[2][rows, :] * factor
        if last:
            result = (accum / total).astype(jnp.bfloat16)
            new[0][:, at : at + HEAD] = result[:BLOCK]
            new[0][:, at + HEAD : at + 2 * HEAD] = result[BLOCK:]
        else:
            new[0][rows, :] = jnp.broadcast_to(top, (2 * BLOCK, HEAD))
            new[1][rows, :] = total
            new[2][rows, :] = accum

    tiles = [(kv, pair) for kv in range(2) for pair in range(GROUP // 2)]
    ahead = scores(*tiles[0])
    pending = None
    for i, tile in enumerate(tiles):
        score = ahead
        if i + 1 < len(tiles):
            ahead = scores(*tiles[i + 1])
        if pending is not None:
            finish(*pending)
        pending = (*weights(score, *tile), *tile)
    finish(*pending)


def attend(core, half, q, b0, blocks, own=False, state=(), last=False):
    vmem = pl.BlockSpec(memory_space=pltpu.VMEM)
    count = own + sum(1 if block.ndim == 3 else 2 for block in blocks)
    keys = 2 * BLOCK * count
    rows = BLOCK * HQ // 2
    if last:
        out_shape = jax.ShapeDtypeStruct(q.shape, jnp.bfloat16)
    else:
        out_shape = [jax.ShapeDtypeStruct((rows, HEAD), jnp.float32)] * 3
    return pl.pallas_call(
        functools.partial(piece, half, own, bool(state), last, 1 + len(blocks)),
        out_shape=out_shape,
        in_specs=[pl.BlockSpec(memory_space=pltpu.SMEM)] + [vmem] * (2 + len(blocks) + len(state)),
        out_specs=vmem if last else [vmem] * 3,
        scratch_shapes=[pltpu.VMEM((2, keys, 2 * HEAD), jnp.bfloat16)] * 2,
        compiler_params=pltpu.CompilerParams(vmem_limit_bytes=32 * 1024 * 1024),
        cost_estimate=pl.CostEstimate(
            flops=8 * rows * keys * HEAD, bytes_accessed=4 << 20, transcendentals=rows * keys
        ),
    )(core, q, b0, *blocks, *state)


def shards(queries, keys, values, doc_ids):
    place = lax.axis_index("sp")
    core, column = place % 2, place // 2 % 4
    first = core == 0

    def section(block, flip, dy=0):
        pairs = [(p * 64 + s, (p + 1) % 8 * 64 + ((s + 8 * dy) % 64 ^ flip)) for p in range(8) for s in range(64)]
        return lax.ppermute(block, ("pp", "sp"), pairs)

    def along_y(block, step0, step1):
        return lax.ppermute(block, "sp", [(s, (s + 8 * (step1 if s % 2 else step0)) % 64) for s in range(64)])

    def even_pair(block):
        return lax.ppermute(block, "sp", [(s, s ^ 2) for s in range(64)])

    def odd_pair(block):
        return lax.ppermute(block, "sp", [(s, s // 8 * 8 + (s + (2 if s & 2 else -2)) % 8) for s in range(64)])

    def swap(block):
        return lax.ppermute(block, "sp", [(s, s ^ 1) for s in range(64)])

    ids = jnp.pad(doc_ids[0].astype(jnp.bfloat16)[None], ((0, 15), (0, 384)))

    def part(j):
        cols = slice(j * 256, (j + 1) * 256)
        return jnp.concatenate([jnp.concatenate([keys[0][:, cols], values[0][:, cols]], axis=1), ids], axis=0)

    half0, half1 = part(0), part(1)
    mine, other = jnp.where(first, half0, half1), jnp.where(first, half1, half0)
    q = queries[0]
    b4 = jnp.stack([section(mine, 0, 1), section(other, 1, 1)])
    qf = section(jnp.where(first, q[:, 2048:], q[:, :2048]), 1)
    qs = section(jnp.where(first, q[:, :2048], q[:, 2048:]), 0)
    (b4,) = lax.optimization_barrier((b4,))
    e1 = even_pair(b4)
    ya = along_y(b4, 1, -1)
    yb = along_y(b4, -1, 1)
    ya, yb, b4, qf, e1 = lax.optimization_barrier((ya, yb, b4, qf, e1))
    f2 = odd_pair(jnp.where((column < 2) == first, yb, ya))
    e2 = even_pair(jnp.where((column % 2 == 0) == first, yb, ya))
    f13 = odd_pair(jnp.stack([b4, e1]))
    b0, b8 = jnp.where(first, yb, ya), jnp.where(first, ya, yb)
    at = core[None].astype(jnp.int32)
    state = attend(at, 1, qf, b0, [b4, b8, e1], own=True)
    f2, *state = lax.optimization_barrier((f2, *state))
    e3 = even_pair(f2)
    state2 = attend(at, 0, qs, b0, [b4, b8, e1, e2, f2], own=True)
    state = attend(at, 1, qf, b0, [e2, f2], state=state)
    e3, f13, qs, qf, b0, *both = lax.optimization_barrier((e3, f13, qs, qf, b0, *state, *state2))
    of_ = attend(at, 1, qf, b0, [e3, f13], state=both[:3], last=True)
    got = swap(of_)
    os_ = attend(at, 0, qs, b0, [e3, f13], state=both[3:], last=True)
    out = jnp.where(first, jnp.concatenate([os_, got], axis=1), jnp.concatenate([got, os_], axis=1))
    return out[None]


def solution(mesh):
    return jax.shard_map(
        shards,
        mesh=mesh,
        in_specs=(P("pp", "sp", None), P("pp", "sp", None), P("pp", "sp", None), P("pp", "sp")),
        out_specs=P("pp", "sp", None),
        check_vma=False,
    )
```

```python
import functools

import jax
import jax.numpy as jnp
from jax import lax
from jax.experimental import pallas as pl
from jax.experimental.pallas import tpu as pltpu
from jax.sharding import PartitionSpec as P

HQ = 32
HK = 4
HEAD = 128
GROUP = HQ // HK
BLOCK = 128
ROWS = BLOCK + 16
SCALE = 1.4426950408889634 / HEAD**0.5
FAR = -131072.0
NT = (((1,), (1,)), ((), ()))


def marks(refs):
    ids = [ref[half, BLOCK : BLOCK + 16, :HEAD][0:1].astype(jnp.float32) for ref in refs for half in range(2)]
    ids = jnp.concatenate(ids, axis=0)
    lane = lax.broadcasted_iota(jnp.int32, ids.shape, 1)
    first = jnp.zeros(ids.shape, jnp.int32)
    last = jnp.zeros(ids.shape, jnp.int32)
    for doc in range(8):
        count = jnp.sum((ids <= doc).astype(jnp.float32), axis=1, keepdims=True).astype(jnp.int32)
        last = jnp.where(lane == doc, count, last)
        first = jnp.where(lane == doc + 1, count, first)
    first = jnp.where(lane > 7, BLOCK, first)
    return first, last


def piece(half, own, carried, last, n_blocks, core_ref, q_ref, *refs):
    b0 = refs[0]
    blocks = []
    for ref in refs[1 - own : n_blocks]:
        blocks.extend([ref] if len(ref.shape) == 3 else [ref.at[0], ref.at[1]])
    refs = refs[n_blocks:]
    old, refs = (refs[:3], refs[3:]) if carried else (None, refs)
    new, (kaug, vaug) = refs[:-2], refs[-2:]
    core = core_ref[0]
    row = lax.broadcasted_iota(jnp.int32, (BLOCK, HEAD), 0)
    lane = lax.broadcasted_iota(jnp.int32, (BLOCK, HEAD), 1)
    first, end = marks([b0] + blocks)
    one = jnp.ones((BLOCK, HEAD), jnp.bfloat16)
    for slot, ref in enumerate(blocks):
        for part in range(2):
            at = (2 * slot + part) * BLOCK
            mark = 2 * slot + part + 2
            inside = (row >= first[mark : mark + 1]) & (row < end[mark : mark + 1])
            hot = jnp.where(inside, 1.0, 0.0).astype(jnp.bfloat16)
            for kv in range(2):
                kaug[kv, at : at + BLOCK, :HEAD] = ref[part, :BLOCK, kv * HEAD : (kv + 1) * HEAD]
                kaug[kv, at : at + BLOCK, HEAD:] = hot
                vaug[kv, at : at + BLOCK, :HEAD] = ref[part, :BLOCK, (2 + kv) * HEAD : (3 + kv) * HEAD]
                vaug[kv, at : at + BLOCK, HEAD:] = one
    inside = (row >= first[half : half + 1]) & (row < end[half : half + 1])
    away = jnp.where(inside | (lane > 7), 0.0, FAR).astype(jnp.bfloat16)
    away = jnp.concatenate([away, away], axis=0)
    if own:
        tall = lax.broadcasted_iota(jnp.int32, (2 * BLOCK, 2 * BLOCK), 0)
        wide = lax.broadcasted_iota(jnp.int32, (2 * BLOCK, 2 * BLOCK), 1)
        qat = (core ^ half) * BLOCK + (tall & (BLOCK - 1))
        kat = (core ^ (wide >> 7)) * BLOCK + (wide & (BLOCK - 1))
        future = kat > qat
    def scores(kv, pair):
        at = (kv * GROUP + 2 * pair) * HEAD
        q2 = jnp.concatenate([q_ref[:, at : at + HEAD], q_ref[:, at + HEAD : at + 2 * HEAD]], axis=0)
        q2 = jnp.concatenate([q2, away], axis=1)
        score = lax.dot_general(q2, kaug[kv], NT, preferred_element_type=jnp.float32)
        if own:
            mine = jnp.where(future, FAR, score[:, : 2 * BLOCK])
            score = mine if len(blocks) == 1 else jnp.concatenate([mine, score[:, 2 * BLOCK :]], axis=1)
        return score

    def weights(score, kv, pair):
        head = kv * GROUP + 2 * pair
        rows = slice(head * BLOCK, (head + 2) * BLOCK)
        top = jnp.max(score, axis=1, keepdims=True)
        factor = None
        if carried:
            before = old[0][rows, :]
            top = jnp.maximum(jnp.broadcast_to(top, before.shape), before)
            factor = jnp.exp2((before - top) * SCALE)
        wide = jnp.concatenate([top] * (2 * len(blocks)), axis=1) if carried else top
        return jnp.exp2((score - wide) * SCALE).astype(jnp.bfloat16), top, factor

    def finish(weight, top, factor, kv, pair):
        head = kv * GROUP + 2 * pair
        at = head * HEAD
        rows = slice(head * BLOCK, (head + 2) * BLOCK)
        both = jnp.dot(weight, vaug[kv], preferred_element_type=jnp.float32)
        total, accum = both[:, HEAD:], both[:, :HEAD]
        if carried:
            total = total + old[1][rows, :] * factor
            accum = accum + old[2][rows, :] * factor
        if last:
            result = (accum / total).astype(jnp.bfloat16)
            new[0][:, at : at + HEAD] = result[:BLOCK]
            new[0][:, at + HEAD : at + 2 * HEAD] = result[BLOCK:]
        else:
            new[0][rows, :] = jnp.broadcast_to(top, (2 * BLOCK, HEAD))
            new[1][rows, :] = total
            new[2][rows, :] = accum

    tiles = [(kv, pair) for kv in range(2) for pair in range(GROUP // 2)]
    ahead = scores(*tiles[0])
    pending = None
    for i, tile in enumerate(tiles):
        score = ahead
        if i + 1 < len(tiles):
            ahead = scores(*tiles[i + 1])
        if pending is not None:
            finish(*pending)
        pending = (*weights(score, *tile), *tile)
    finish(*pending)


def attend(core, half, q, b0, blocks, own=False, state=(), last=False):
    vmem = pl.BlockSpec(memory_space=pltpu.VMEM)
    count = own + sum(1 if block.ndim == 3 else 2 for block in blocks)
    keys = 2 * BLOCK * count
    rows = BLOCK * HQ // 2
    if last:
        out_shape = jax.ShapeDtypeStruct(q.shape, jnp.bfloat16)
    else:
        out_shape = [jax.ShapeDtypeStruct((rows, HEAD), jnp.float32)] * 3
    return pl.pallas_call(
        functools.partial(piece, half, own, bool(state), last, 1 + len(blocks)),
        out_shape=out_shape,
        in_specs=[pl.BlockSpec(memory_space=pltpu.SMEM)] + [vmem] * (2 + len(blocks) + len(state)),
        out_specs=vmem if last else [vmem] * 3,
        scratch_shapes=[pltpu.VMEM((2, keys, 2 * HEAD), jnp.bfloat16)] * 2,
        compiler_params=pltpu.CompilerParams(vmem_limit_bytes=32 * 1024 * 1024),
        cost_estimate=pl.CostEstimate(
            flops=8 * rows * keys * HEAD, bytes_accessed=4 << 20, transcendentals=rows * keys
        ),
    )(core, q, b0, *blocks, *state)


def shards(queries, keys, values, doc_ids):
    place = lax.axis_index("sp")
    core, column = place % 2, place // 2 % 4
    first = core == 0

    def section(block, flip, dy=0):
        pairs = [(p * 64 + s, (p + 1) % 8 * 64 + ((s + 8 * dy) % 64 ^ flip)) for p in range(8) for s in range(64)]
        return lax.ppermute(block, ("pp", "sp"), pairs)

    def along_y(block, step0, step1):
        return lax.ppermute(block, "sp", [(s, (s + 8 * (step1 if s % 2 else step0)) % 64) for s in range(64)])

    def even_pair(block):
        return lax.ppermute(block, "sp", [(s, s ^ 2) for s in range(64)])

    def odd_pair(block):
        return lax.ppermute(block, "sp", [(s, s // 8 * 8 + (s + (2 if s & 2 else -2)) % 8) for s in range(64)])

    def swap(block):
        return lax.ppermute(block, "sp", [(s, s ^ 1) for s in range(64)])

    ids = jnp.pad(doc_ids[0].astype(jnp.bfloat16)[None], ((0, 15), (0, 384)))

    def part(j):
        cols = slice(j * 256, (j + 1) * 256)
        return jnp.concatenate([jnp.concatenate([keys[0][:, cols], values[0][:, cols]], axis=1), ids], axis=0)

    half0, half1 = part(0), part(1)
    mine, other = jnp.where(first, half0, half1), jnp.where(first, half1, half0)
    q = queries[0]
    b4 = jnp.stack([section(mine, 0, 1), section(other, 1, 1)])
    qf = section(jnp.where(first, q[:, 2048:], q[:, :2048]), 1)
    qs = section(jnp.where(first, q[:, :2048], q[:, 2048:]), 0)
    (b4,) = lax.optimization_barrier((b4,))
    e1 = even_pair(b4)
    ya = along_y(b4, 1, -1)
    yb = along_y(b4, -1, 1)
    ya, yb, b4, qf = lax.optimization_barrier((ya, yb, b4, qf))
    f2 = odd_pair(jnp.where((column < 2) == first, yb, ya))
    e2 = even_pair(jnp.where((column % 2 == 0) == first, yb, ya))
    f13 = odd_pair(jnp.stack([b4, e1]))
    b0, b8 = jnp.where(first, yb, ya), jnp.where(first, ya, yb)
    at = core[None].astype(jnp.int32)
    state = attend(at, 1, qf, b0, [b4, b8, e1], own=True)
    f2, *state = lax.optimization_barrier((f2, *state))
    e3 = even_pair(f2)
    state2 = attend(at, 0, qs, b0, [b4, b8, e1, e2, f2], own=True)
    state = attend(at, 1, qf, b0, [e2, f2], state=state)
    e3, f13, qs, qf, b0, *both = lax.optimization_barrier((e3, f13, qs, qf, b0, *state, *state2))
    of_ = attend(at, 1, qf, b0, [e3, f13], state=both[:3], last=True)
    got = swap(of_)
    os_ = attend(at, 0, qs, b0, [e3, f13], state=both[3:], last=True)
    out = jnp.where(first, jnp.concatenate([os_, got], axis=1), jnp.concatenate([got, os_], axis=1))
    return out[None]


def solution(mesh):
    return jax.shard_map(
        shards,
        mesh=mesh,
        in_specs=(P("pp", "sp", None), P("pp", "sp", None), P("pp", "sp", None), P("pp", "sp")),
        out_specs=P("pp", "sp", None),
        check_vma=False,
    )
```

```python
import functools

import jax
import jax.numpy as jnp
from jax import lax
from jax.experimental import pallas as pl
from jax.experimental.pallas import tpu as pltpu
from jax.sharding import PartitionSpec as P

HQ = 32
HK = 4
HEAD = 128
GROUP = HQ // HK
BLOCK = 128
ROWS = BLOCK + 16
SCALE = 1.4426950408889634 / HEAD**0.5
FAR = -131072.0
NT = (((1,), (1,)), ((), ()))


def marks(refs):
    ids = [ref[half, BLOCK : BLOCK + 16, :HEAD][0:1].astype(jnp.float32) for ref in refs for half in range(2)]
    ids = jnp.concatenate(ids, axis=0)
    lane = lax.broadcasted_iota(jnp.int32, ids.shape, 1)
    first = jnp.zeros(ids.shape, jnp.int32)
    last = jnp.zeros(ids.shape, jnp.int32)
    for doc in range(8):
        count = jnp.sum((ids <= doc).astype(jnp.float32), axis=1, keepdims=True).astype(jnp.int32)
        last = jnp.where(lane == doc, count, last)
        first = jnp.where(lane == doc + 1, count, first)
    first = jnp.where(lane > 7, BLOCK, first)
    return first, last


def piece(half, own, carried, last, n_blocks, core_ref, q_ref, *refs):
    b0 = refs[0]
    blocks = []
    for ref in refs[1 - own : n_blocks]:
        blocks.extend([ref] if len(ref.shape) == 3 else [ref.at[0], ref.at[1]])
    refs = refs[n_blocks:]
    old, refs = (refs[:3], refs[3:]) if carried else (None, refs)
    new, (kaug, vaug) = refs[:-2], refs[-2:]
    core = core_ref[0]
    row = lax.broadcasted_iota(jnp.int32, (BLOCK, HEAD), 0)
    lane = lax.broadcasted_iota(jnp.int32, (BLOCK, HEAD), 1)
    first, end = marks([b0] + blocks)
    one = jnp.ones((BLOCK, HEAD), jnp.bfloat16)
    for slot, ref in enumerate(blocks):
        for part in range(2):
            at = (2 * slot + part) * BLOCK
            mark = 2 * slot + part + 2
            inside = (row >= first[mark : mark + 1]) & (row < end[mark : mark + 1])
            hot = jnp.where(inside, 1.0, 0.0).astype(jnp.bfloat16)
            for kv in range(2):
                kaug[kv, at : at + BLOCK, :HEAD] = ref[part, :BLOCK, kv * HEAD : (kv + 1) * HEAD]
                kaug[kv, at : at + BLOCK, HEAD:] = hot
                vaug[kv, at : at + BLOCK, :HEAD] = ref[part, :BLOCK, (2 + kv) * HEAD : (3 + kv) * HEAD]
                vaug[kv, at : at + BLOCK, HEAD:] = one
    inside = (row >= first[half : half + 1]) & (row < end[half : half + 1])
    away = jnp.where(inside | (lane > 7), 0.0, FAR).astype(jnp.bfloat16)
    away = jnp.concatenate([away, away], axis=0)
    if own:
        tall = lax.broadcasted_iota(jnp.int32, (2 * BLOCK, 2 * BLOCK), 0)
        wide = lax.broadcasted_iota(jnp.int32, (2 * BLOCK, 2 * BLOCK), 1)
        qat = (core ^ half) * BLOCK + (tall & (BLOCK - 1))
        kat = (core ^ (wide >> 7)) * BLOCK + (wide & (BLOCK - 1))
        future = kat > qat
    def scores(kv, pair):
        at = (kv * GROUP + 2 * pair) * HEAD
        q2 = jnp.concatenate([q_ref[:, at : at + HEAD], q_ref[:, at + HEAD : at + 2 * HEAD]], axis=0)
        q2 = jnp.concatenate([q2, away], axis=1)
        score = lax.dot_general(q2, kaug[kv], NT, preferred_element_type=jnp.float32)
        if own:
            mine = jnp.where(future, FAR, score[:, : 2 * BLOCK])
            score = mine if len(blocks) == 1 else jnp.concatenate([mine, score[:, 2 * BLOCK :]], axis=1)
        return score

    def weights(score, kv, pair):
        head = kv * GROUP + 2 * pair
        rows = slice(head * BLOCK, (head + 2) * BLOCK)
        top = jnp.max(score, axis=1, keepdims=True)
        factor = None
        if carried:
            before = old[0][rows, :]
            top = jnp.maximum(jnp.broadcast_to(top, before.shape), before)
            factor = jnp.exp2((before - top) * SCALE)
        wide = jnp.concatenate([top] * (2 * len(blocks)), axis=1) if carried else top
        return jnp.exp2((score - wide) * SCALE).astype(jnp.bfloat16), top, factor

    def finish(weight, top, factor, kv, pair):
        head = kv * GROUP + 2 * pair
        at = head * HEAD
        rows = slice(head * BLOCK, (head + 2) * BLOCK)
        both = jnp.dot(weight, vaug[kv], preferred_element_type=jnp.float32)
        total, accum = both[:, HEAD:], both[:, :HEAD]
        if carried:
            total = total + old[1][rows, :] * factor
            accum = accum + old[2][rows, :] * factor
        if last:
            result = (accum / total).astype(jnp.bfloat16)
            new[0][:, at : at + HEAD] = result[:BLOCK]
            new[0][:, at + HEAD : at + 2 * HEAD] = result[BLOCK:]
        else:
            new[0][rows, :] = jnp.broadcast_to(top, (2 * BLOCK, HEAD))
            new[1][rows, :] = total
            new[2][rows, :] = accum

    tiles = [(kv, pair) for kv in range(2) for pair in range(GROUP // 2)]
    ahead = scores(*tiles[0])
    pending = None
    for i, tile in enumerate(tiles):
        score = ahead
        if i + 1 < len(tiles):
            ahead = scores(*tiles[i + 1])
        if pending is not None:
            finish(*pending)
        pending = (*weights(score, *tile), *tile)
    finish(*pending)


def attend(core, half, q, b0, blocks, own=False, state=(), last=False):
    vmem = pl.BlockSpec(memory_space=pltpu.VMEM)
    count = own + sum(1 if block.ndim == 3 else 2 for block in blocks)
    keys = 2 * BLOCK * count
    rows = BLOCK * HQ // 2
    if last:
        out_shape = jax.ShapeDtypeStruct(q.shape, jnp.bfloat16)
    else:
        out_shape = [jax.ShapeDtypeStruct((rows, HEAD), jnp.float32)] * 3
    return pl.pallas_call(
        functools.partial(piece, half, own, bool(state), last, 1 + len(blocks)),
        out_shape=out_shape,
        in_specs=[pl.BlockSpec(memory_space=pltpu.SMEM)] + [vmem] * (2 + len(blocks) + len(state)),
        out_specs=vmem if last else [vmem] * 3,
        scratch_shapes=[pltpu.VMEM((2, keys, 2 * HEAD), jnp.bfloat16)] * 2,
        compiler_params=pltpu.CompilerParams(vmem_limit_bytes=32 * 1024 * 1024),
        cost_estimate=pl.CostEstimate(
            flops=8 * rows * keys * HEAD, bytes_accessed=4 << 20, transcendentals=rows * keys
        ),
    )(core, q, b0, *blocks, *state)


def shards(queries, keys, values, doc_ids):
    place = lax.axis_index("sp")
    core, column = place % 2, place // 2 % 4
    first = core == 0

    def section(block, flip, dy=0):
        pairs = [(p * 64 + s, (p + 1) % 8 * 64 + ((s + 8 * dy) % 64 ^ flip)) for p in range(8) for s in range(64)]
        return lax.ppermute(block, ("pp", "sp"), pairs)

    def along_y(block, step0, step1):
        return lax.ppermute(block, "sp", [(s, (s + 8 * (step1 if s % 2 else step0)) % 64) for s in range(64)])

    def even_pair(block):
        return lax.ppermute(block, "sp", [(s, s ^ 2) for s in range(64)])

    def odd_pair(block):
        return lax.ppermute(block, "sp", [(s, s // 8 * 8 + (s + (2 if s & 2 else -2)) % 8) for s in range(64)])

    def swap(block):
        return lax.ppermute(block, "sp", [(s, s ^ 1) for s in range(64)])

    ids = jnp.pad(doc_ids[0].astype(jnp.bfloat16)[None], ((0, 15), (0, 384)))

    def part(j):
        cols = slice(j * 256, (j + 1) * 256)
        return jnp.concatenate([jnp.concatenate([keys[0][:, cols], values[0][:, cols]], axis=1), ids], axis=0)

    half0, half1 = part(0), part(1)
    mine, other = jnp.where(first, half0, half1), jnp.where(first, half1, half0)
    q = queries[0]
    b4 = jnp.stack([section(mine, 0, 1), section(other, 1, 1)])
    qf = section(jnp.where(first, q[:, 2048:], q[:, :2048]), 1)
    qs = section(jnp.where(first, q[:, :2048], q[:, 2048:]), 0)
    (b4,) = lax.optimization_barrier((b4,))
    e1 = even_pair(b4)
    ya = along_y(b4, 1, -1)
    yb = along_y(b4, -1, 1)
    ya, yb, b4, qf = lax.optimization_barrier((ya, yb, b4, qf))
    f2 = odd_pair(jnp.where((column < 2) == first, yb, ya))
    e2 = even_pair(jnp.where((column % 2 == 0) == first, yb, ya))
    f13 = odd_pair(jnp.stack([b4, e1]))
    b0, b8 = jnp.where(first, yb, ya), jnp.where(first, ya, yb)
    at = core[None].astype(jnp.int32)
    state = attend(at, 1, qf, b0, [b4, b8, e1], own=True)
    (f2,) = lax.optimization_barrier((f2,))
    e3 = even_pair(f2)
    state2 = attend(at, 0, qs, b0, [b4, b8, e1, e2, f2], own=True)
    state = attend(at, 1, qf, b0, [e2, f2], state=state)
    e3, f13, qs, qf, b0, *both = lax.optimization_barrier((e3, f13, qs, qf, b0, *state, *state2))
    of_ = attend(at, 1, qf, b0, [e3, f13], state=both[:3], last=True)
    got = swap(of_)
    os_ = attend(at, 0, qs, b0, [e3, f13], state=both[3:], last=True)
    out = jnp.where(first, jnp.concatenate([os_, got], axis=1), jnp.concatenate([got, os_], axis=1))
    return out[None]


def solution(mesh):
    return jax.shard_map(
        shards,
        mesh=mesh,
        in_specs=(P("pp", "sp", None), P("pp", "sp", None), P("pp", "sp", None), P("pp", "sp")),
        out_specs=P("pp", "sp", None),
        check_vma=False,
    )
```

```python
import functools

import jax
import jax.numpy as jnp
from jax import lax
from jax.experimental import pallas as pl
from jax.experimental.pallas import tpu as pltpu
from jax.sharding import PartitionSpec as P

HQ = 32
HK = 4
HEAD = 128
GROUP = HQ // HK
BLOCK = 128
ROWS = BLOCK + 16
SCALE = 1.4426950408889634 / HEAD**0.5
FAR = -131072.0
NT = (((1,), (1,)), ((), ()))


def pack(core_ref, k_ref, v_ref, ids_ref, mine_ref, other_ref, ids_vmem, sems):
    half = 2 * HEAD
    copies = [pltpu.make_async_copy(ids_ref, ids_vmem, sems.at[4])]
    for i, ref in enumerate((mine_ref, other_ref)):
        cols = pl.ds(pl.multiple_of((core_ref[0] ^ i) * half, half), half)
        for j, source in enumerate((k_ref, v_ref)):
            target = ref.at[:BLOCK, j * half : (j + 1) * half]
            copies.append(pltpu.make_async_copy(source.at[:, cols], target, sems.at[2 * i + j]))
    for copy in copies:
        copy.start()
    copies[0].wait()
    row = lax.broadcasted_iota(jnp.int32, (16, HEAD), 0)
    ids = jnp.where(row == 0, ids_vmem[...].astype(jnp.float32), 0.0).astype(jnp.bfloat16)
    for ref in (mine_ref, other_ref):
        ref[BLOCK:, :HEAD] = ids
        ref[BLOCK:, HEAD:] = jnp.zeros((16, 3 * HEAD), jnp.bfloat16)
    for copy in copies[1:]:
        copy.wait()


def packed(core, keys, values, ids):
    vmem = pl.BlockSpec(memory_space=pltpu.VMEM)
    hbm = pl.BlockSpec(memory_space=pltpu.HBM)
    return pl.pallas_call(
        pack,
        out_shape=[jax.ShapeDtypeStruct((ROWS, 4 * HEAD), jnp.bfloat16)] * 2,
        in_specs=[pl.BlockSpec(memory_space=pltpu.SMEM)] + [hbm] * 3,
        out_specs=[vmem] * 2,
        scratch_shapes=[pltpu.VMEM(ids.shape, jnp.int32), pltpu.SemaphoreType.DMA((5,))],
        compiler_params=pltpu.CompilerParams(vmem_limit_bytes=8 * 1024 * 1024),
    )(core, keys, values, ids)


def marks(refs):
    ids = [ref[half, BLOCK : BLOCK + 16, :HEAD][0:1].astype(jnp.float32) for ref in refs for half in range(2)]
    ids = jnp.concatenate(ids, axis=0)
    lane = lax.broadcasted_iota(jnp.int32, ids.shape, 1)
    first = jnp.zeros(ids.shape, jnp.int32)
    last = jnp.zeros(ids.shape, jnp.int32)
    for doc in range(8):
        count = jnp.sum((ids <= doc).astype(jnp.float32), axis=1, keepdims=True).astype(jnp.int32)
        last = jnp.where(lane == doc, count, last)
        first = jnp.where(lane == doc + 1, count, first)
    first = jnp.where(lane > 7, BLOCK, first)
    return first, last


def place(core, half, part, parts):
    width = HQ * HEAD // 2 // parts
    return pl.ds(pl.multiple_of((core ^ half) * (HQ * HEAD // 2) + part * width, width), width)


def piece(half, own, carried, last, n_blocks, core_ref, q_ref, *refs):
    b0 = refs[0]
    blocks = []
    for ref in refs[1 - own : n_blocks]:
        blocks.extend([ref] if len(ref.shape) == 3 else [ref.at[0], ref.at[1]])
    refs = refs[n_blocks:]
    old, refs = (refs[:3], refs[3:]) if carried else (None, refs)
    core = core_ref[0]
    ends = last and half == 0
    if ends:
        out, *new, kaug, vaug, sems = refs
        copies = [
            pltpu.make_async_copy(
                new[0].at[:, part * (GROUP * HEAD) : (part + 1) * (GROUP * HEAD)],
                out.at[:, place(core, 0, part, 2)],
                sems.at[part],
            )
            for part in range(2)
        ]
    else:
        *new, kaug, vaug = refs
    row = lax.broadcasted_iota(jnp.int32, (BLOCK, HEAD), 0)
    lane = lax.broadcasted_iota(jnp.int32, (BLOCK, HEAD), 1)
    first, end = marks([b0] + blocks)
    one = jnp.ones((BLOCK, HEAD), jnp.bfloat16)
    for slot, ref in enumerate(blocks):
        for part in range(2):
            at = (2 * slot + part) * BLOCK
            mark = 2 * slot + part + 2
            inside = (row >= first[mark : mark + 1]) & (row < end[mark : mark + 1])
            hot = jnp.where(inside, 1.0, 0.0).astype(jnp.bfloat16)
            for kv in range(2):
                kaug[kv, at : at + BLOCK, :HEAD] = ref[part, :BLOCK, kv * HEAD : (kv + 1) * HEAD]
                kaug[kv, at : at + BLOCK, HEAD:] = hot
                vaug[kv, at : at + BLOCK, :HEAD] = ref[part, :BLOCK, (2 + kv) * HEAD : (3 + kv) * HEAD]
                vaug[kv, at : at + BLOCK, HEAD:] = one
    inside = (row >= first[half : half + 1]) & (row < end[half : half + 1])
    away = jnp.where(inside | (lane > 7), 0.0, FAR).astype(jnp.bfloat16)
    away = jnp.concatenate([away, away], axis=0)
    if own:
        tall = lax.broadcasted_iota(jnp.int32, (2 * BLOCK, 2 * BLOCK), 0)
        wide = lax.broadcasted_iota(jnp.int32, (2 * BLOCK, 2 * BLOCK), 1)
        qat = (core ^ half) * BLOCK + (tall & (BLOCK - 1))
        kat = (core ^ (wide >> 7)) * BLOCK + (wide & (BLOCK - 1))
        future = kat > qat
    def scores(kv, pair):
        at = (kv * GROUP + 2 * pair) * HEAD
        q2 = jnp.concatenate([q_ref[:, at : at + HEAD], q_ref[:, at + HEAD : at + 2 * HEAD]], axis=0)
        q2 = jnp.concatenate([q2, away], axis=1)
        score = lax.dot_general(q2, kaug[kv], NT, preferred_element_type=jnp.float32)
        if own:
            mine = jnp.where(future, FAR, score[:, : 2 * BLOCK])
            score = mine if len(blocks) == 1 else jnp.concatenate([mine, score[:, 2 * BLOCK :]], axis=1)
        return score

    def weights(score, kv, pair):
        head = kv * GROUP + 2 * pair
        rows = slice(head * BLOCK, (head + 2) * BLOCK)
        top = jnp.max(score, axis=1, keepdims=True)
        factor = None
        if carried:
            before = old[0][rows, :]
            top = jnp.maximum(jnp.broadcast_to(top, before.shape), before)
            factor = jnp.exp2((before - top) * SCALE)
        wide = jnp.concatenate([top] * (2 * len(blocks)), axis=1) if carried else top
        return jnp.exp2((score - wide) * SCALE).astype(jnp.bfloat16), top, factor

    def finish(weight, top, factor, kv, pair):
        head = kv * GROUP + 2 * pair
        at = head * HEAD
        rows = slice(head * BLOCK, (head + 2) * BLOCK)
        both = jnp.dot(weight, vaug[kv], preferred_element_type=jnp.float32)
        total, accum = both[:, HEAD:], both[:, :HEAD]
        if carried:
            total = total + old[1][rows, :] * factor
            accum = accum + old[2][rows, :] * factor
        if last:
            result = (accum / total).astype(jnp.bfloat16)
            new[0][:, at : at + HEAD] = result[:BLOCK]
            new[0][:, at + HEAD : at + 2 * HEAD] = result[BLOCK:]
        else:
            new[0][rows, :] = jnp.broadcast_to(top, (2 * BLOCK, HEAD))
            new[1][rows, :] = total
            new[2][rows, :] = accum

    tiles = [(kv, pair) for kv in range(2) for pair in range(GROUP // 2)]
    ahead = scores(*tiles[0])
    pending = None
    for i, tile in enumerate(tiles):
        score = ahead
        if i + 1 < len(tiles):
            ahead = scores(*tiles[i + 1])
        if pending is not None:
            finish(*pending)
        if ends and i == len(tiles) // 2:
            copies[0].start()
        pending = (*weights(score, *tile), *tile)
    finish(*pending)
    if ends:
        copies[1].start()
        copies[0].wait()
        copies[1].wait()


def fill(core_ref, got, old, out, sem):
    copy = pltpu.make_async_copy(got, out.at[:, place(core_ref[0], 1, 0, 1)], sem)
    copy.start()
    copy.wait()


def filled(core, got, out):
    hbm = pl.BlockSpec(memory_space=pl.ANY)
    return pl.pallas_call(
        fill,
        out_shape=jax.ShapeDtypeStruct(out.shape, out.dtype),
        in_specs=[pl.BlockSpec(memory_space=pltpu.SMEM), pl.BlockSpec(memory_space=pltpu.VMEM), hbm],
        out_specs=hbm,
        scratch_shapes=[pltpu.SemaphoreType.DMA],
        input_output_aliases={2: 0},
        compiler_params=pltpu.CompilerParams(vmem_limit_bytes=8 * 1024 * 1024),
    )(core, got, out)


def attend(core, half, q, b0, blocks, own=False, state=(), last=False):
    vmem = pl.BlockSpec(memory_space=pltpu.VMEM)
    count = own + sum(1 if block.ndim == 3 else 2 for block in blocks)
    keys = 2 * BLOCK * count
    rows = BLOCK * HQ // 2
    ends = last and half == 0
    out_spec = vmem
    scratch = [pltpu.VMEM((2, keys, 2 * HEAD), jnp.bfloat16)] * 2
    if ends:
        out_shape = jax.ShapeDtypeStruct((BLOCK, HQ * HEAD), jnp.bfloat16)
        out_spec = pl.BlockSpec(memory_space=pl.ANY)
        scratch = [pltpu.VMEM(q.shape, jnp.bfloat16)] + scratch + [pltpu.SemaphoreType.DMA((2,))]
    elif last:
        out_shape = jax.ShapeDtypeStruct(q.shape, jnp.bfloat16)
    else:
        out_shape = [jax.ShapeDtypeStruct((rows, HEAD), jnp.float32)] * 3
    return pl.pallas_call(
        functools.partial(piece, half, own, bool(state), last, 1 + len(blocks)),
        out_shape=out_shape,
        in_specs=[pl.BlockSpec(memory_space=pltpu.SMEM)] + [vmem] * (2 + len(blocks) + len(state)),
        out_specs=out_spec if last else [vmem] * 3,
        scratch_shapes=scratch,
        compiler_params=pltpu.CompilerParams(vmem_limit_bytes=32 * 1024 * 1024),
        cost_estimate=pl.CostEstimate(
            flops=8 * rows * keys * HEAD, bytes_accessed=4 << 20, transcendentals=rows * keys
        ),
    )(core, q, b0, *blocks, *state)


def shards(queries, keys, values, doc_ids):
    place = lax.axis_index("sp")
    core, column = place % 2, place // 2 % 4
    first = core == 0

    def section(block, flip, dy=0):
        pairs = [(p * 64 + s, (p + 1) % 8 * 64 + ((s + 8 * dy) % 64 ^ flip)) for p in range(8) for s in range(64)]
        return lax.ppermute(block, ("pp", "sp"), pairs)

    def along_y(block, step0, step1):
        return lax.ppermute(block, "sp", [(s, (s + 8 * (step1 if s % 2 else step0)) % 64) for s in range(64)])

    def even_pair(block):
        return lax.ppermute(block, "sp", [(s, s ^ 2) for s in range(64)])

    def odd_pair(block):
        return lax.ppermute(block, "sp", [(s, s // 8 * 8 + (s + (2 if s & 2 else -2)) % 8) for s in range(64)])

    def swap(block):
        return lax.ppermute(block, "sp", [(s, s ^ 1) for s in range(64)])

    at = core[None].astype(jnp.int32)
    mine, other = packed(at, keys[0], values[0], doc_ids)
    q = queries[0]
    b4 = jnp.stack([section(mine, 0, 1), section(other, 1, 1)])
    qf = section(jnp.where(first, q[:, 2048:], q[:, :2048]), 1)
    qs = section(jnp.where(first, q[:, :2048], q[:, 2048:]), 0)
    (b4,) = lax.optimization_barrier((b4,))
    e1 = even_pair(b4)
    ya = along_y(b4, 1, -1)
    yb = along_y(b4, -1, 1)
    ya, yb, b4, qf = lax.optimization_barrier((ya, yb, b4, qf))
    f2 = odd_pair(jnp.where((column < 2) == first, yb, ya))
    e2 = even_pair(jnp.where((column % 2 == 0) == first, yb, ya))
    f13 = odd_pair(jnp.stack([b4, e1]))
    b0, b8 = jnp.where(first, yb, ya), jnp.where(first, ya, yb)
    state = attend(at, 1, qf, b0, [b4, b8, e1], own=True)
    (f2,) = lax.optimization_barrier((f2,))
    e3 = even_pair(f2)
    state2 = attend(at, 0, qs, b0, [b4, b8, e1, e2, f2], own=True)
    state = attend(at, 1, qf, b0, [e2, f2], state=state)
    e3, *state = lax.optimization_barrier((e3, *state, *state2))
    state, state2 = state[:3], state[3:]
    state = attend(at, 1, qf, b0, [e3], state=state)
    e3, f13, qs, qf, b0, *both = lax.optimization_barrier((e3, f13, qs, qf, b0, *state, *state2))
    of_ = attend(at, 1, qf, b0, [f13], state=both[:3], last=True)
    got = swap(of_)
    os_ = attend(at, 0, qs, b0, [e3, f13], state=both[3:], last=True)
    out = filled(at, got, os_)
    return out[None]


def solution(mesh):
    return jax.shard_map(
        shards,
        mesh=mesh,
        in_specs=(P("pp", "sp", None), P("pp", "sp", None), P("pp", "sp", None), P("pp", "sp")),
        out_specs=P("pp", "sp", None),
        check_vma=False,
    )
```

```python
import functools

import jax
import jax.numpy as jnp
from jax import lax
from jax.experimental import pallas as pl
from jax.experimental.pallas import tpu as pltpu
from jax.sharding import PartitionSpec as P

HQ = 32
HK = 4
HEAD = 128
GROUP = HQ // HK
BLOCK = 128
ROWS = BLOCK + 16
SCALE = 1.4426950408889634 / HEAD**0.5
FAR = -131072.0
NT = (((1,), (1,)), ((), ()))


def marks(q_ref, refs):
    ids = [q_ref[0:16, HQ // 2 * HEAD :][0:1].astype(jnp.float32)]
    ids += [ref[half, BLOCK : BLOCK + 16, :HEAD][0:1].astype(jnp.float32) for ref in refs for half in range(2)]
    ids = jnp.concatenate(ids, axis=0)
    lane = lax.broadcasted_iota(jnp.int32, ids.shape, 1)
    first = jnp.zeros(ids.shape, jnp.int32)
    last = jnp.zeros(ids.shape, jnp.int32)
    for doc in range(8):
        count = jnp.sum((ids <= doc).astype(jnp.float32), axis=1, keepdims=True).astype(jnp.int32)
        last = jnp.where(lane == doc, count, last)
        first = jnp.where(lane == doc + 1, count, first)
    first = jnp.where(lane > 7, BLOCK, first)
    return first, last


def piece(half, own, carried, last, n_blocks, core_ref, q_ref, *refs):
    blocks = []
    for ref in refs[:n_blocks]:
        blocks.extend([ref] if len(ref.shape) == 3 else [ref.at[0], ref.at[1]])
    refs = refs[n_blocks:]
    old, refs = (refs[:3], refs[3:]) if carried else (None, refs)
    new, (kaug, vaug) = refs[:-2], refs[-2:]
    core = core_ref[0]
    row = lax.broadcasted_iota(jnp.int32, (BLOCK, HEAD), 0)
    lane = lax.broadcasted_iota(jnp.int32, (BLOCK, HEAD), 1)
    first, end = marks(q_ref, blocks)
    one = jnp.ones((BLOCK, HEAD), jnp.bfloat16)
    for slot, ref in enumerate(blocks):
        for part in range(2):
            at = (2 * slot + part) * BLOCK
            mark = 2 * slot + part + 1
            inside = (row >= first[mark : mark + 1]) & (row < end[mark : mark + 1])
            hot = jnp.where(inside, 1.0, 0.0).astype(jnp.bfloat16)
            for kv in range(2):
                kaug[kv, at : at + BLOCK, :HEAD] = ref[part, :BLOCK, kv * HEAD : (kv + 1) * HEAD]
                kaug[kv, at : at + BLOCK, HEAD:] = hot
                vaug[kv, at : at + BLOCK, :HEAD] = ref[part, :BLOCK, (2 + kv) * HEAD : (3 + kv) * HEAD]
                vaug[kv, at : at + BLOCK, HEAD:] = one
    inside = (row >= first[0:1]) & (row < end[0:1])
    away = jnp.where(inside | (lane > 7), 0.0, FAR).astype(jnp.bfloat16)
    away = jnp.concatenate([away, away], axis=0)
    if own:
        tall = lax.broadcasted_iota(jnp.int32, (2 * BLOCK, 2 * BLOCK), 0)
        wide = lax.broadcasted_iota(jnp.int32, (2 * BLOCK, 2 * BLOCK), 1)
        qat = (core ^ half) * BLOCK + (tall & (BLOCK - 1))
        kat = (core ^ (wide >> 7)) * BLOCK + (wide & (BLOCK - 1))
        future = [kat - (1 - core_ref[flag]) * 2 * BLOCK > qat for flag in own]
    def scores(kv, pair):
        at = (kv * GROUP + 2 * pair) * HEAD
        q2 = jnp.concatenate([q_ref[:, at : at + HEAD], q_ref[:, at + HEAD : at + 2 * HEAD]], axis=0)
        q2 = jnp.concatenate([q2, away], axis=1)
        score = lax.dot_general(q2, kaug[kv], NT, preferred_element_type=jnp.float32)
        if own:
            wide = 2 * BLOCK
            parts = [jnp.where(late, FAR, score[:, i * wide : (i + 1) * wide]) for i, late in enumerate(future)]
            if len(own) < len(blocks):
                parts.append(score[:, len(own) * wide :])
            score = parts[0] if len(parts) == 1 else jnp.concatenate(parts, axis=1)
        return score

    def weights(score, kv, pair):
        head = kv * GROUP + 2 * pair
        rows = slice(head * BLOCK, (head + 2) * BLOCK)
        top = jnp.max(score, axis=1, keepdims=True)
        factor = None
        if carried:
            before = old[0][rows, :]
            top = jnp.maximum(jnp.broadcast_to(top, before.shape), before)
            factor = jnp.exp2((before - top) * SCALE)
        wide = jnp.concatenate([top] * (2 * len(blocks)), axis=1) if carried else top
        return jnp.exp2((score - wide) * SCALE).astype(jnp.bfloat16), top, factor

    def finish(weight, top, factor, kv, pair):
        head = kv * GROUP + 2 * pair
        at = head * HEAD
        rows = slice(head * BLOCK, (head + 2) * BLOCK)
        both = jnp.dot(weight, vaug[kv], preferred_element_type=jnp.float32)
        total, accum = both[:, HEAD:], both[:, :HEAD]
        if carried:
            total = total + old[1][rows, :] * factor
            accum = accum + old[2][rows, :] * factor
        if last:
            result = (accum / total).astype(jnp.bfloat16)
            new[0][:, at : at + HEAD] = result[:BLOCK]
            new[0][:, at + HEAD : at + 2 * HEAD] = result[BLOCK:]
        else:
            new[0][rows, :] = jnp.broadcast_to(top, (2 * BLOCK, HEAD))
            new[1][rows, :] = total
            new[2][rows, :] = accum

    tiles = [(kv, pair) for kv in range(2) for pair in range(GROUP // 2)]
    ahead = scores(*tiles[0])
    pending = None
    for i, tile in enumerate(tiles):
        score = ahead
        if i + 1 < len(tiles):
            ahead = scores(*tiles[i + 1])
        if pending is not None:
            finish(*pending)
        pending = (*weights(score, *tile), *tile)
    finish(*pending)


def attend(core, half, q, blocks, own=(), state=(), last=False):
    vmem = pl.BlockSpec(memory_space=pltpu.VMEM)
    count = sum(1 if block.ndim == 3 else 2 for block in blocks)
    keys = 2 * BLOCK * count
    rows = BLOCK * HQ // 2
    if last:
        out_shape = jax.ShapeDtypeStruct((BLOCK, HQ // 2 * HEAD), jnp.bfloat16)
    else:
        out_shape = [jax.ShapeDtypeStruct((rows, HEAD), jnp.float32)] * 3
    return pl.pallas_call(
        functools.partial(piece, half, own, bool(state), last, len(blocks)),
        out_shape=out_shape,
        in_specs=[pl.BlockSpec(memory_space=pltpu.SMEM)] + [vmem] * (1 + len(blocks) + len(state)),
        out_specs=vmem if last else [vmem] * 3,
        scratch_shapes=[pltpu.VMEM((2, keys, 2 * HEAD), jnp.bfloat16)] * 2,
        compiler_params=pltpu.CompilerParams(vmem_limit_bytes=32 * 1024 * 1024),
        cost_estimate=pl.CostEstimate(
            flops=8 * rows * keys * HEAD, bytes_accessed=4 << 20, transcendentals=rows * keys
        ),
    )(core, q, *blocks, *state)


def shards(queries, keys, values, doc_ids):
    place = lax.axis_index("sp")
    core, column = place % 2, place // 2 % 4
    first = core == 0

    def section(block, flip, dy=0):
        pairs = [(p * 64 + s, (p + 1) % 8 * 64 + ((s + 8 * dy) % 64 ^ flip)) for p in range(8) for s in range(64)]
        return lax.ppermute(block, ("pp", "sp"), pairs)

    def along_y(block, steps):
        return lax.ppermute(block, "sp", [(s, (s + 8 * steps[s // 2 % 4]) % 64) for s in range(64)])

    def even_pair(block):
        return lax.ppermute(block, "sp", [(s, s ^ 2) for s in range(64)])

    def odd_pair(block):
        return lax.ppermute(block, "sp", [(s, s // 8 * 8 + (s + (2 if s & 2 else -2)) % 8) for s in range(64)])

    def swap(block):
        return lax.ppermute(block, "sp", [(s, s ^ 1) for s in range(64)])

    ids = jnp.pad(doc_ids[0].astype(jnp.bfloat16)[None], ((0, 15), (0, 384)))

    def part(j):
        cols = slice(j * 256, (j + 1) * 256)
        return jnp.concatenate([jnp.concatenate([keys[0][:, cols], values[0][:, cols]], axis=1), ids], axis=0)

    half0, half1 = part(0), part(1)
    mine, other = jnp.where(first, half0, half1), jnp.where(first, half1, half0)
    q = queries[0]
    b4 = jnp.stack([section(mine, 0, 1), section(other, 1, 1)])
    rider = jnp.pad(doc_ids[0].astype(jnp.bfloat16)[None], ((0, BLOCK - 1), (0, 0)))
    qf = section(jnp.concatenate([jnp.where(first, q[:, 2048:], q[:, :2048]), rider], axis=1), 1)
    qs = section(jnp.concatenate([jnp.where(first, q[:, :2048], q[:, 2048:]), rider], axis=1), 0)
    (b4,) = lax.optimization_barrier((b4,))
    ya = along_y(b4, (-1, -1, 1, 1))
    e1 = even_pair(b4)
    ya, b4, qf = lax.optimization_barrier((ya, b4, qf))
    f2 = odd_pair(ya)
    e1, ya = lax.optimization_barrier((e1, ya))
    e2 = along_y(e1, (1, -1, 1, -1))
    f13 = odd_pair(jnp.stack([b4, e1]))
    left = (column < 2).astype(jnp.int32)
    at = jnp.stack([core.astype(jnp.int32), left, 1 - left])
    state = attend(at, 1, qf, [ya, b4, e1], own=(1,))
    f2, b5 = lax.optimization_barrier((f2, b4))
    e3 = even_pair(f2)
    yb = along_y(b5, (1, 1, -1, -1))
    state2 = attend(at, 0, qs, [ya, b4, e1, f2, e2], own=(1,))
    state = attend(at, 1, qf, [f2, e2], state=state)
    yb, f13, *both = lax.optimization_barrier((yb, f13, *state, *state2))
    state = attend(at, 1, qf, [yb, f13], own=(2,), state=both[:3])
    e3, yb, f13, qs, qf, *both = lax.optimization_barrier((e3, yb, f13, qs, qf, *state, *both[3:]))
    of_ = attend(at, 1, qf, [e3], state=both[:3], last=True)
    got = swap(of_)
    os_ = attend(at, 0, qs, [yb, e3, f13], own=(2,), state=both[3:], last=True)
    out = jnp.where(first, jnp.concatenate([os_, got], axis=1), jnp.concatenate([got, os_], axis=1))
    return out[None]


def solution(mesh):
    return jax.shard_map(
        shards,
        mesh=mesh,
        in_specs=(P("pp", "sp", None), P("pp", "sp", None), P("pp", "sp", None), P("pp", "sp")),
        out_specs=P("pp", "sp", None),
        check_vma=False,
    )
```

```python
import functools

import jax
import jax.numpy as jnp
from jax import lax
from jax.experimental import pallas as pl
from jax.experimental.pallas import tpu as pltpu
from jax.sharding import PartitionSpec as P

HQ = 32
HK = 4
HEAD = 128
GROUP = HQ // HK
BLOCK = 128
ROWS = BLOCK + 16
SCALE = 1.4426950408889634 / HEAD**0.5
FAR = -131072.0
NT = (((1,), (1,)), ((), ()))


def marks(refs):
    ids = [ref[half, BLOCK : BLOCK + 16, :HEAD][0:1].astype(jnp.float32) for ref in refs for half in range(2)]
    ids = jnp.concatenate(ids, axis=0)
    lane = lax.broadcasted_iota(jnp.int32, ids.shape, 1)
    first = jnp.zeros(ids.shape, jnp.int32)
    last = jnp.zeros(ids.shape, jnp.int32)
    for doc in range(8):
        count = jnp.sum((ids <= doc).astype(jnp.float32), axis=1, keepdims=True).astype(jnp.int32)
        last = jnp.where(lane == doc, count, last)
        first = jnp.where(lane == doc + 1, count, first)
    first = jnp.where(lane > 7, BLOCK, first)
    return first, last


def piece(half, own, carried, last, n_blocks, core_ref, q_ref, *refs):
    b0 = refs[0]
    blocks = []
    for ref in refs[1 - own : n_blocks]:
        blocks.extend([ref] if len(ref.shape) == 3 else [ref.at[0], ref.at[1]])
    refs = refs[n_blocks:]
    old, refs = (refs[:3], refs[3:]) if carried else (None, refs)
    new, (kaug, vaug) = refs[:-2], refs[-2:]
    core = core_ref[0]
    row = lax.broadcasted_iota(jnp.int32, (BLOCK, HEAD), 0)
    lane = lax.broadcasted_iota(jnp.int32, (BLOCK, HEAD), 1)
    first, end = marks([b0] + blocks)
    one = jnp.ones((BLOCK, HEAD), jnp.bfloat16)
    for slot, ref in enumerate(blocks):
        for part in range(2):
            at = (2 * slot + part) * BLOCK
            mark = 2 * slot + part + 2
            inside = (row >= first[mark : mark + 1]) & (row < end[mark : mark + 1])
            hot = jnp.where(inside, 1.0, 0.0).astype(jnp.bfloat16)
            for kv in range(2):
                kaug[kv, at : at + BLOCK, :HEAD] = ref[part, :BLOCK, kv * HEAD : (kv + 1) * HEAD]
                kaug[kv, at : at + BLOCK, HEAD:] = hot
                vaug[kv, at : at + BLOCK, :HEAD] = ref[part, :BLOCK, (2 + kv) * HEAD : (3 + kv) * HEAD]
                vaug[kv, at : at + BLOCK, HEAD:] = one
    inside = (row >= first[half : half + 1]) & (row < end[half : half + 1])
    away = jnp.where(inside | (lane > 7), 0.0, FAR).astype(jnp.bfloat16)
    away = jnp.concatenate([away, away], axis=0)
    if own:
        tall = lax.broadcasted_iota(jnp.int32, (2 * BLOCK, 2 * BLOCK), 0)
        wide = lax.broadcasted_iota(jnp.int32, (2 * BLOCK, 2 * BLOCK), 1)
        qat = (core ^ half) * BLOCK + (tall & (BLOCK - 1))
        kat = (core ^ (wide >> 7)) * BLOCK + (wide & (BLOCK - 1))
        future = kat > qat
    def scores(kv, pair):
        at = (kv * GROUP + 2 * pair) * HEAD
        q2 = jnp.concatenate([q_ref[:, at : at + HEAD], q_ref[:, at + HEAD : at + 2 * HEAD]], axis=0)
        q2 = jnp.concatenate([q2, away], axis=1)
        score = lax.dot_general(q2, kaug[kv], NT, preferred_element_type=jnp.float32)
        if own:
            mine = jnp.where(future, FAR, score[:, : 2 * BLOCK])
            score = mine if len(blocks) == 1 else jnp.concatenate([mine, score[:, 2 * BLOCK :]], axis=1)
        return score

    def weights(score, kv, pair):
        head = kv * GROUP + 2 * pair
        rows = slice(head * BLOCK, (head + 2) * BLOCK)
        top = jnp.max(score, axis=1, keepdims=True)
        factor = None
        if carried:
            before = old[0][rows, :]
            top = jnp.maximum(jnp.broadcast_to(top, before.shape), before)
            factor = jnp.exp2((before - top) * SCALE)
        wide = jnp.concatenate([top] * (2 * len(blocks)), axis=1) if carried else top
        return jnp.exp2((score - wide) * SCALE).astype(jnp.bfloat16), top, factor

    def finish(weight, top, factor, kv, pair):
        head = kv * GROUP + 2 * pair
        at = head * HEAD
        rows = slice(head * BLOCK, (head + 2) * BLOCK)
        both = jnp.dot(weight, vaug[kv], preferred_element_type=jnp.float32)
        total, accum = both[:, HEAD:], both[:, :HEAD]
        if carried:
            total = total + old[1][rows, :] * factor
            accum = accum + old[2][rows, :] * factor
        if last:
            result = (accum / total).astype(jnp.bfloat16)
            new[0][:, at : at + HEAD] = result[:BLOCK]
            new[0][:, at + HEAD : at + 2 * HEAD] = result[BLOCK:]
        else:
            new[0][rows, :] = jnp.broadcast_to(top, (2 * BLOCK, HEAD))
            new[1][rows, :] = total
            new[2][rows, :] = accum

    tiles = [(kv, pair) for kv in range(2) for pair in range(GROUP // 2)]
    ahead = scores(*tiles[0])
    pending = None
    for i, tile in enumerate(tiles):
        score = ahead
        if i + 1 < len(tiles):
            ahead = scores(*tiles[i + 1])
        if pending is not None:
            finish(*pending)
        pending = (*weights(score, *tile), *tile)
    finish(*pending)


def attend(core, half, q, b0, blocks, own=False, state=(), last=False):
    vmem = pl.BlockSpec(memory_space=pltpu.VMEM)
    count = own + sum(1 if block.ndim == 3 else 2 for block in blocks)
    keys = 2 * BLOCK * count
    rows = BLOCK * HQ // 2
    if last:
        out_shape = jax.ShapeDtypeStruct(q.shape, jnp.bfloat16)
    else:
        out_shape = [jax.ShapeDtypeStruct((rows, HEAD), jnp.float32)] * 3
    return pl.pallas_call(
        functools.partial(piece, half, own, bool(state), last, 1 + len(blocks)),
        out_shape=out_shape,
        in_specs=[pl.BlockSpec(memory_space=pltpu.SMEM)] + [vmem] * (2 + len(blocks) + len(state)),
        out_specs=vmem if last else [vmem] * 3,
        scratch_shapes=[pltpu.VMEM((2, keys, 2 * HEAD), jnp.bfloat16)] * 2,
        compiler_params=pltpu.CompilerParams(vmem_limit_bytes=32 * 1024 * 1024),
        cost_estimate=pl.CostEstimate(
            flops=8 * rows * keys * HEAD, bytes_accessed=4 << 20, transcendentals=rows * keys
        ),
    )(core, q, b0, *blocks, *state)


def shards(queries, keys, values, doc_ids):
    place = lax.axis_index("sp")
    core, column = place % 2, place // 2 % 4
    first = core == 0

    def section(block, flip, dy=0):
        pairs = [(p * 64 + s, (p + 1) % 8 * 64 + ((s + 8 * dy) % 64 ^ flip)) for p in range(8) for s in range(64)]
        return lax.ppermute(block, ("pp", "sp"), pairs)

    def along_y(block, step0, step1):
        return lax.ppermute(block, "sp", [(s, (s + 8 * (step1 if s % 2 else step0)) % 64) for s in range(64)])

    def even_pair(block):
        return lax.ppermute(block, "sp", [(s, s ^ 2) for s in range(64)])

    def odd_pair(block):
        return lax.ppermute(block, "sp", [(s, s // 8 * 8 + (s + (2 if s & 2 else -2)) % 8) for s in range(64)])

    def swap(block):
        return lax.ppermute(block, "sp", [(s, s ^ 1) for s in range(64)])

    ids = jnp.pad(doc_ids[0].astype(jnp.bfloat16)[None], ((0, 15), (0, 384)))

    def part(j):
        cols = slice(j * 256, (j + 1) * 256)
        return jnp.concatenate([jnp.concatenate([keys[0][:, cols], values[0][:, cols]], axis=1), ids], axis=0)

    half0, half1 = part(0), part(1)
    mine, other = jnp.where(first, half0, half1), jnp.where(first, half1, half0)
    q = queries[0]
    b4 = jnp.stack([section(mine, 0, 1), section(other, 1, 1)])
    qf = section(jnp.where(first, q[:, 2048:], q[:, :2048]), 1)
    qs = section(jnp.where(first, q[:, :2048], q[:, 2048:]), 0)
    (b4,) = lax.optimization_barrier((b4,))
    e1 = even_pair(b4)
    ya = along_y(b4, 1, -1)
    yb = along_y(b4, -1, 1)
    ya, yb, b4, qf = lax.optimization_barrier((ya, yb, b4, qf))
    f2 = odd_pair(jnp.where((column < 2) == first, yb, ya))
    e2 = even_pair(jnp.where((column % 2 == 0) == first, yb, ya))
    f13 = odd_pair(jnp.stack([b4, e1]))
    b0, b8 = jnp.where(first, yb, ya), jnp.where(first, ya, yb)
    at = core[None].astype(jnp.int32)
    state = attend(at, 1, qf, b0, [b4, b8, e1], own=True)
    (f2,) = lax.optimization_barrier((f2,))
    e3 = even_pair(f2)
    state2 = attend(at, 0, qs, b0, [b4, b8, e1, e2, f2], own=True)
    state = attend(at, 1, qf, b0, [e2, f2], state=state)
    e3, *state = lax.optimization_barrier((e3, *state, *state2))
    state, state2 = state[:3], state[3:]
    state = attend(at, 1, qf, b0, [e3], state=state)
    e3, f13, qs, qf, b0, *both = lax.optimization_barrier((e3, f13, qs, qf, b0, *state, *state2))
    of_ = attend(at, 1, qf, b0, [f13], state=both[:3], last=True)
    got = swap(of_)
    os_ = attend(at, 0, qs, b0, [e3, f13], state=both[3:], last=True)
    out = jnp.where(first, jnp.concatenate([os_, got], axis=1), jnp.concatenate([got, os_], axis=1))
    return out[None]


def solution(mesh):
    return jax.shard_map(
        shards,
        mesh=mesh,
        in_specs=(P("pp", "sp", None), P("pp", "sp", None), P("pp", "sp", None), P("pp", "sp")),
        out_specs=P("pp", "sp", None),
        check_vma=False,
    )
```
